128 devices in a mesh: ulysses: 4 (over z), blk: 8 (over y, core), tensor: 4 (over x).
Axes of the slice: x: 4, y: 4, z: 4, core: 2. Of those that a mesh axis runs over, the one named last changes fastest.
Arguments:
- tokens: bfloat16 [8192, 5120], P(('ulysses', 'blk'), 'tensor'), may hold values from -20 to 20
- w_qkv: bfloat16 [5120, 3, 4096], P(None, None, ('ulysses', 'tensor')), may hold values from -2 to 2
- qkv_scale: float32 [3, 32], P(None, ('ulysses', 'tensor')), may hold values from 0.6 to 9
- block_mask: int32 [32, 64, 64], P(('ulysses', 'tensor')), may hold values from 0 to 1, as said below
- w_out: bfloat16 [4, 1024, 5120], P(None, 'tensor'), may hold values from -0.125 to 0.125
Outputs:
- mixed: bfloat16 [8192, 5120], P(('ulysses', 'blk'), 'tensor')
The draws below stay inside these ranges and needn't reach their ends.
Inputs may be any that keep to these rules, and one draw needn't show every extreme that they name: `block_mask`: 0 or 1; the share of ones differs from head to head.
All inputs are finite; a program needn't handle non-finite values.
Results may differ from the reference program's by a relative error of at most 0.015.
Values may be sent and summed in bfloat16 or wider, within the bound.
No kernel may reach another device: no remote copies, remote signals or barrier semaphores. Data moves between devices by JAX's collectives and lax.ppermute only.
A program may use at most 128 MiB of HBM per device.

```python
import math
import jax
import jax.numpy as jnp
from jax import lax

D = 5120
HD = 128
HPD = 2
BLOCK = 128
HEADS = 32
TOKENS = 8192
NB = 64
N_ULYSSES = 4
N_TENSOR = 4


def draw_block_mask(key, part):
    dense_key = jax.random.fold_in(key, 11)
    cell_key = jax.random.fold_in(key, 12)
    density = jax.random.randint(dense_key, (HEADS, 1, 1), 1, 8)
    cells = jax.random.randint(cell_key, (HEADS, NB, NB), 0, 8)
    return (cells < density).astype(jnp.int32)


def head_law(key):
    order_key = jax.random.fold_in(key, 21)
    base_key = jax.random.fold_in(key, 22)
    strong_key = jax.random.fold_in(key, 23)
    temper_key = jax.random.fold_in(key, 24)
    coupling_key = jax.random.fold_in(key, 25)
    ranking = jax.random.permutation(order_key, HEADS)
    strong = ranking < HEADS // 4
    base = jnp.exp(jax.random.uniform(base_key, (3, HEADS), jnp.float32, jnp.log(0.6), jnp.log(2.0)))
    high = jnp.exp(jax.random.uniform(strong_key, (3, HEADS), jnp.float32, jnp.log(5.0), jnp.log(9.0)))
    query_key_rows = (jnp.arange(3, dtype=jnp.int32) < 2)[:, None]
    chosen = jnp.where(query_key_rows & strong[None, :], high, base).astype(jnp.float32)
    temper = jnp.exp(jax.random.uniform(temper_key, (HEADS,), jnp.float32, jnp.log(0.8), jnp.log(2.0)))
    coupling = jax.random.uniform(coupling_key, (HEADS,), jnp.float32, 0.75, 1.0)
    return (chosen, temper, coupling)


def draw_qkv_scale(key, part):
    chosen, temper, coupling = head_law(key)
    return chosen


def draw_w_qkv(key, part):
    chosen, temper, coupling = head_law(key)
    column_gain = jnp.sqrt(temper / (chosen[0] * chosen[1]))
    query_key = jax.random.fold_in(key, 31)
    other_key = jax.random.fold_in(key, 32)
    value_key = jax.random.fold_in(key, 33)
    shape = (D, HEADS * HD)
    query_noise = jax.random.truncated_normal(query_key, -4.0, 4.0, shape, jnp.float32)
    other_noise = jax.random.truncated_normal(other_key, -4.0, 4.0, shape, jnp.float32)
    value_noise = jax.random.truncated_normal(value_key, -4.0, 4.0, shape, jnp.float32)
    head_gain = jnp.repeat(column_gain, HD)[None, :]
    head_coupling = jnp.repeat(coupling, HD)[None, :]
    spread = 1.0 / jnp.sqrt(jnp.float32(D))
    query_cols = head_gain * query_noise * spread
    key_cols = head_gain * (head_coupling * query_noise + jnp.sqrt(1.0 - head_coupling * head_coupling) * other_noise) * spread
    value_cols = value_noise * spread
    return jnp.stack([query_cols, key_cols, value_cols], axis=1).astype(jnp.bfloat16)


def draw_tokens(key, part):
    noise_key = jax.random.fold_in(key, 41)
    direction_key = jax.random.fold_in(key, 42)
    member_key = jax.random.fold_in(key, 43)
    polarity_key = jax.random.fold_in(key, 44)
    strength_key = jax.random.fold_in(key, 45)
    noise = jax.random.truncated_normal(noise_key, -4.0, 4.0, (TOKENS, D), jnp.float32)
    largest = 2.5
    directions = jax.random.truncated_normal(direction_key, -4.0, 4.0, (16, D), jnp.float32)
    member = jax.random.randint(member_key, (TOKENS,), 0, 16)
    polarity = jnp.where(jax.random.randint(polarity_key, (TOKENS,), 0, 2) == 1, 1.0, -1.0)
    strength = jax.random.uniform(strength_key, (TOKENS,), jnp.float32, 0.0, largest)
    shared = jnp.take(directions, member, axis=0)
    return (noise + (polarity * strength)[:, None] * shared).astype(jnp.bfloat16)


def block_scale(stream_key, dims, pieces, low, high):
    loudness, own = 1.0, jax.random.fold_in(stream_key, 6)
    for dim, blocks in pieces:
        heights = jnp.exp(jax.random.uniform(jax.random.fold_in(own, dim), (blocks,), jnp.float32, low / len(pieces), high / len(pieces)))
        loudness = loudness * jnp.repeat(heights, dims[dim] // blocks).reshape([-1 if axis == dim else 1 for axis in range(len(dims))])
    return loudness


def gaussian(stream_key, extent, scale, most, split=(), held_as=jnp.bfloat16):
    result = scale * jax.random.normal(stream_key, extent, jnp.float32)
    if split:
        result = result * block_scale(stream_key, extent, split, -0.22, 0.18)
    return jnp.clip(result, -most, most).astype(held_as)


def setup_inputs(seed: int = 0) -> dict:
    seeds = jax.random.split(jax.random.key(seed), 6)
    return {
        "tokens": draw_tokens(jax.random.fold_in(seeds[5], 71), 0),
        "w_qkv": draw_w_qkv(jax.random.fold_in(seeds[5], 71), 0),
        "qkv_scale": draw_qkv_scale(jax.random.fold_in(seeds[5], 71), 0),
        "block_mask": draw_block_mask(jax.random.fold_in(seeds[5], 71), 0),
        "w_out": gaussian(seeds[4], (N_ULYSSES, N_TENSOR * HPD * HD, D), (HPD * HD * 8) ** -0.5, 0.125, ((1, 4),)),
    }


def attend_head(queries, keys, values, head_mask):
    key_blocks = jnp.arange(TOKENS, dtype=jnp.int32) // BLOCK
    score_scale = 1.0 / math.sqrt(HD)

    def one_block(position):
        query_rows = lax.dynamic_slice_in_dim(queries, (position * BLOCK).astype(jnp.int32), BLOCK, 0)
        scores = jnp.dot(query_rows, keys.T, preferred_element_type=jnp.float32) * score_scale
        allowed = (head_mask[position][key_blocks] == 1) | (key_blocks == position)
        scores = jnp.where(allowed[None, :], scores, -jnp.inf)
        highest = lax.optimization_barrier(jnp.max(scores, axis=-1, keepdims=True))
        weights = jnp.exp(scores - highest)
        denominator = lax.optimization_barrier(jnp.sum(weights, axis=-1, keepdims=True))
        summed = jnp.dot(weights.astype(jnp.bfloat16), values, preferred_element_type=jnp.float32)
        return summed / denominator
    return lax.map(one_block, jnp.arange(NB, dtype=jnp.int32))

def reference(tokens, w_qkv, qkv_scale, block_mask, w_out):
    matrix = w_qkv.reshape(D, 3 * HEADS * HD)
    projected = jnp.dot(tokens, matrix, preferred_element_type=jnp.float32).reshape(TOKENS, 3, HEADS, HD)
    projected = (projected * qkv_scale[None, :, :, None]).astype(jnp.bfloat16)

    def per_head(head_index):
        return attend_head(projected[:, 0, head_index], projected[:, 1, head_index], projected[:, 2, head_index], block_mask[head_index])
    attended = lax.map(per_head, jnp.arange(HEADS, dtype=jnp.int32))
    attended = attended.astype(jnp.bfloat16).reshape(HEADS, TOKENS, HD)
    attended = jnp.transpose(attended, (1, 0, 2)).reshape(TOKENS, HEADS * HD)
    mixed = jnp.dot(attended, w_out.reshape(HEADS * HD, D), preferred_element_type=jnp.float32)
    return mixed.astype(jnp.bfloat16)
```

```python
import functools
import math

import jax
import jax.numpy as jnp
from jax import lax
from jax.experimental import pallas as pl
from jax.experimental.pallas import tpu as pltpu
from jax.sharding import PartitionSpec as P

HD = 128
BLOCK = 128
NEG = -1e30
LOG2E = 1.4426950408889634
OFFSETS = (0, -1, 1, 2)
CONTRACT_LAST = (((1,), (1,)), ((), ()))


def ring(n, step):
    return [(i, (i + step) % n) for i in range(n)]


def y_ring(n, step):
    return [(i, (i + 2 * step) % n) for i in range(n)]


def core_swap(n):
    return [(i, i ^ 1) for i in range(n)]


def attn_kernel(bk, q_ref, qm_ref, *refs):
    kv_refs, o_ref = refs[:-1], refs[-1]
    rows = q_ref.shape[0]
    q = jnp.concatenate([q_ref[...], qm_ref[...]], axis=1)
    tiles = [(r, j) for r in range(len(kv_refs)) for j in range(kv_refs[r].shape[0] // bk)]
    lane = lax.broadcasted_iota(jnp.int32, (bk, HD), 1)
    inner = lax.broadcasted_iota(jnp.int32, (bk, HD), 0) // BLOCK
    ones = (lane == 0).astype(jnp.float32).astype(jnp.bfloat16)
    per_tile = bk // BLOCK

    def score(i):
        r, j = tiles[i]
        onehot = (lane == inner + i * per_tile).astype(jnp.float32).astype(jnp.bfloat16)
        k = jnp.concatenate([kv_refs[r][j * bk : (j + 1) * bk, :HD], onehot], axis=1)
        return lax.dot_general(q, k, CONTRACT_LAST, preferred_element_type=jnp.float32)

    high = jnp.full((rows, 1), -3e38, jnp.float32)
    acc = jnp.zeros((rows, 2 * HD), jnp.float32)
    s = score(0)
    for i in range(len(tiles)):
        s_next = score(i + 1) if i + 1 < len(tiles) else None
        new_high = jnp.maximum(high, jnp.max(s, axis=1, keepdims=True))
        p = jnp.exp2(s - new_high).astype(jnp.bfloat16)
        factor = jnp.exp2(high - new_high)
        r, j = tiles[i]
        v = jnp.concatenate([kv_refs[r][j * bk : (j + 1) * bk, HD:], ones], axis=1)
        acc = acc * factor + jnp.dot(p, v, preferred_element_type=jnp.float32)
        high = new_high
        s = s_next
    o_ref[...] = (acc[:, :HD] / acc[:, HD : HD + 1]).astype(jnp.bfloat16)


def attention(q, qm, kvs, bq=512, bk=512):
    rows = q.shape[0]
    keys = sum(kv.shape[0] for kv in kvs)
    return pl.pallas_call(
        functools.partial(attn_kernel, bk),
        grid=(rows // bq,),
        in_specs=[pl.BlockSpec((bq, HD), lambda i: (i, 0)), pl.BlockSpec((bq, HD), lambda i: (i, 0))]
        + [pl.BlockSpec(kv.shape, lambda i: (0, 0)) for kv in kvs],
        out_specs=pl.BlockSpec((bq, HD), lambda i: (i, 0)),
        out_shape=jax.ShapeDtypeStruct((rows, HD), jnp.bfloat16),
        compiler_params=pltpu.CompilerParams(vmem_limit_bytes=48 << 20),
        cost_estimate=pl.CostEstimate(
            flops=8 * rows * keys * HD, bytes_accessed=keys * 512, transcendentals=rows * keys
        ),
    )(q, qm, *kvs)


def local(tokens, w_qkv, qkv_scale, block_mask, w_out):
    nu, nb, nt = lax.axis_size("ulysses"), lax.axis_size("blk"), lax.axis_size("tensor")
    u, b, t = lax.axis_index("ulysses"), lax.axis_index("blk"), lax.axis_index("tensor")
    y, core = b // 2, b % 2
    feat = tokens.shape[1]
    half = tokens.shape[0] // 2
    quarter = half // 2
    pp = lax.ppermute

    def direct(value, axis, n):
        return [value] + [pp(value, axis, ring(n, s)) for s in (1, -1, 2)]

    w_rel = [
        lax.dynamic_slice_in_dim(w_qkv, ((t + o) % nt) * feat, feat, 0) for o in OFFSETS
    ]
    scale = qkv_scale * jnp.array([LOG2E / math.sqrt(HD), 1.0, 1.0], jnp.float32)[:, None]

    a_own = jnp.concatenate(direct(tokens[:half], "tensor", nt), axis=1)
    b_own = jnp.concatenate(direct(tokens[half:], "ulysses", nu), axis=0)

    a_m = pp(a_own, "ulysses", ring(nu, 1))
    b_m = pp(b_own, "tensor", ring(nt, 1))
    a_p = pp(a_own, "ulysses", ring(nu, -1))
    b_p = pp(b_own, "tensor", ring(nt, -1))
    a_opp = jnp.concatenate(
        [
            pp(a_m[:quarter], "ulysses", ring(nu, 1)),
            pp(a_p[quarter:], "ulysses", ring(nu, -1)),
        ],
        axis=0,
    )
    bh = b_own.shape[0] // 2
    b_opp = jnp.concatenate(
        [pp(b_m[:bh], "tensor", ring(nt, 1)), pp(b_p[bh:], "tensor", ring(nt, -1))], axis=0
    )

    def project(value, w):
        return jnp.einsum("rd,dcn->rcn", value, w, preferred_element_type=jnp.float32)

    w_full = jnp.concatenate(w_rel, axis=0)

    def finish(acc):
        rows = acc.shape[0]
        full = acc.reshape(rows, 3, 2, HD) * scale[None, :, :, None]
        full = full.astype(jnp.bfloat16)
        keep = lax.dynamic_index_in_dim(full, core, 2, keepdims=False)
        give = lax.dynamic_index_in_dim(full, 1 - core, 2, keepdims=False)
        got = pp(give.reshape(rows, 3 * HD), "blk", core_swap(nb))
        both = jnp.concatenate([keep.reshape(rows, 3 * HD), got], axis=0)
        kv = lax.all_gather(
            both[:, HD:],
            "blk",
            axis=0,
            tiled=True,
            axis_index_groups=[list(range(0, nb, 2)), list(range(1, nb, 2))],
        )
        return both[:, :HD], kv

    acc_a = jnp.concatenate([project(v, w_full) for v in (a_own, a_m, a_p, a_opp)], axis=0)
    q_a, kv_a = finish(acc_a)
    acc_b = sum(project(v, w) for v, w in zip((b_own, b_m, b_p, b_opp), w_rel))
    q_b, kv_b = finish(acc_b)

    groups = (u + jnp.array(OFFSETS, jnp.int32)) % nu
    cores = jnp.stack([core, 1 - core])

    def block_ids(ys, odd):
        return (
            ((groups[None, None, :] * nb + 2 * ys[:, None, None] + cores[None, :, None]) * 2 + odd)
        ).reshape(-1)

    all_y = jnp.arange(nb // 2, dtype=jnp.int32)
    key_ids = jnp.concatenate([block_ids(all_y, 0), block_ids(all_y, 1)])
    query_ids = jnp.concatenate([block_ids(y[None], 0), block_ids(y[None], 1)])
    blocks = jnp.arange(block_mask.shape[1], dtype=jnp.int32)
    key_hot = (key_ids[:, None] == blocks[None, :]).astype(jnp.float32)
    query_hot = (query_ids[:, None] == blocks[None, :]).astype(jnp.float32)
    mask = lax.dynamic_index_in_dim(block_mask, core, 0, keepdims=False).astype(jnp.float32)
    live = query_hot @ mask @ key_hot.T > 0.5
    live = live | (query_ids[:, None] == key_ids[None, :])
    bias = jnp.where(live, 0.0, NEG).astype(jnp.bfloat16)
    bias = jnp.pad(bias, ((0, 0), (0, HD - bias.shape[1])))
    bias = jnp.repeat(bias, BLOCK, axis=0)

    out = attention(jnp.concatenate([q_a, q_b], axis=0), bias, [kv_a, kv_b])

    out = out.reshape(2, 2, nu, half, HD)
    other = pp(out[:, 1], "blk", core_swap(nb))
    mine = out[:, 0]
    first = jnp.where(core == 0, mine, other)
    second = jnp.where(core == 0, other, mine)
    heads = jnp.concatenate([first, second], axis=-1)
    heads = heads.transpose(1, 0, 2, 3).reshape(nu, 2 * half, 2 * HD)
    arrived = [heads[0]] + [
        pp(heads[i], "ulysses", ring(nu, OFFSETS[i])) for i in range(1, nu)
    ]
    partial_value = sum(
        jnp.dot(
            v,
            lax.dynamic_index_in_dim(w_out, (u - o) % nu, 0, keepdims=False),
            preferred_element_type=jnp.float32,
        )
        for v, o in zip(arrived, OFFSETS)
    )
    return lax.psum_scatter(
        partial_value.astype(jnp.bfloat16), "tensor", scatter_dimension=1, tiled=True
    )


def solution(mesh):
    return jax.shard_map(
        local,
        mesh=mesh,
        in_specs=(
            P(("ulysses", "blk"), "tensor"),
            P(None, None, ("ulysses", "tensor")),
            P(None, ("ulysses", "tensor")),
            P(("ulysses", "tensor"), None, None),
            P(None, "tensor", None),
        ),
        out_specs=P(("ulysses", "blk"), "tensor"),
        check_vma=False,
    )
```

```python
import functools
import math

import jax
import jax.numpy as jnp
from jax import lax
from jax.experimental import pallas as pl
from jax.experimental.pallas import tpu as pltpu
from jax.sharding import PartitionSpec as P

HD = 128
BLOCK = 128
NEG = -1e30
LOG2E = 1.4426950408889634
OFFSETS = (0, -1, 1, 2)
CONTRACT_LAST = (((1,), (1,)), ((), ()))


def ring(n, step):
    return [(i, (i + step) % n) for i in range(n)]


def y_ring(n, step):
    return [(i, (i + 2 * step) % n) for i in range(n)]


def core_swap(n):
    return [(i, i ^ 1) for i in range(n)]


def project_tile(x, w_ref, acc_ref, rows):
    for c in range(3):
        acc_ref[rows, c * 256 : (c + 1) * 256] += jnp.dot(
            x, w_ref[c], preferred_element_type=jnp.float32
        )


def emit_heads(acc, scale_ref, core, q_ref, kv_ref, give_ref):
    scaled = (acc * scale_ref[...]).astype(jnp.bfloat16)
    heads = [[scaled[:, c * 256 + h * HD : c * 256 + (h + 1) * HD] for c in range(3)] for h in (0, 1)]
    is_first = core == 0

    @pl.when(is_first)
    def _():
        q_ref[...] = heads[0][0]
        kv_ref[...] = jnp.concatenate(heads[0][1:], axis=1)
        give_ref[...] = jnp.concatenate(heads[1], axis=1)

    @pl.when(jnp.logical_not(is_first))
    def _():
        q_ref[...] = heads[1][0]
        kv_ref[...] = jnp.concatenate(heads[1][1:], axis=1)
        give_ref[...] = jnp.concatenate(heads[0], axis=1)


def heads_shape(rows):
    return [jax.ShapeDtypeStruct((rows, n * HD), jnp.bfloat16) for n in (1, 2, 3)]


def heads_specs(rows):
    return [pl.BlockSpec((rows, n * HD), lambda r, s: (0, 0)) for n in (1, 2, 3)]


def rows_kernel(sizes, where_ref, w_ref, scale_ref, *refs):
    xs, outs, acc_ref = refs[: len(sizes)], refs[len(sizes) : -1], refs[-1]
    r = pl.program_id(0)

    @pl.when(r == 0)
    def _():
        acc_ref[...] = jnp.zeros_like(acc_ref)

    start = 0
    for x_ref, n in zip(xs, sizes):
        project_tile(x_ref[...], w_ref, acc_ref, slice(start, start + n))
        start += n

    @pl.when(r == pl.num_programs(0) - 1)
    def _():
        emit_heads(acc_ref[...], scale_ref, where_ref[4], *outs)


def project_rows(where, w, scale, xs):
    sizes = [x.shape[0] for x in xs]
    rows, feat = sum(sizes), xs[0].shape[1] // 4
    return pl.pallas_call(
        functools.partial(rows_kernel, sizes),
        grid_spec=pltpu.PrefetchScalarGridSpec(
            num_scalar_prefetch=1,
            grid=(4,),
            in_specs=[
                pl.BlockSpec((3, feat, 256), lambda r, s: (0, s[r], 0)),
                pl.BlockSpec((1, 768), lambda r, s: (0, 0)),
            ]
            + [pl.BlockSpec((n, feat), lambda r, s: (0, r)) for n in sizes],
            out_specs=heads_specs(rows),
            scratch_shapes=[pltpu.VMEM((rows, 768), jnp.float32)],
        ),
        out_shape=heads_shape(rows),
        compiler_params=pltpu.CompilerParams(vmem_limit_bytes=40 << 20),
        cost_estimate=pl.CostEstimate(
            flops=2 * rows * 4 * feat * 768, bytes_accessed=w.size * 2, transcendentals=0
        ),
    )(where, w, scale, *xs)


def part_kernel(where_ref, w_ref, *refs):
    xs, acc_ref = refs[:-1], refs[-1]
    r = pl.program_id(0)

    @pl.when(r == 0)
    def _():
        acc_ref[...] = jnp.zeros_like(acc_ref)

    for i, x_ref in enumerate(xs):

        @pl.when(r == i)
        def _():
            project_tile(x_ref[...], w_ref, acc_ref, slice(None))


def project_part(where, w, xs):
    rows, feat = xs[0].shape
    return pl.pallas_call(
        part_kernel,
        grid_spec=pltpu.PrefetchScalarGridSpec(
            num_scalar_prefetch=1,
            grid=(len(xs),),
            in_specs=[pl.BlockSpec((3, feat, 256), lambda r, s: (0, s[r], 0))]
            + [pl.BlockSpec((rows, feat), lambda r, s: (0, 0)) for _ in xs],
            out_specs=pl.BlockSpec((rows, 768), lambda r, s: (0, 0)),
        ),
        out_shape=jax.ShapeDtypeStruct((rows, 768), jnp.float32),
        compiler_params=pltpu.CompilerParams(vmem_limit_bytes=40 << 20),
        cost_estimate=pl.CostEstimate(
            flops=2 * rows * len(xs) * feat * 768, bytes_accessed=6 << 20, transcendentals=0
        ),
    )(where, w, *xs)


def last_kernel(na, nb, where_ref, w_ref, scale_ref, a0, a1, b0, b1, part_ref, *refs):
    outs, acc_ref = refs[:-1], refs[-1]
    r = pl.program_id(0)

    @pl.when(r == 0)
    def _():
        acc_ref[:na] = jnp.zeros((na, 768), jnp.float32)
        acc_ref[na:] = part_ref[...]

    project_tile(a0[...], w_ref, acc_ref, slice(0, na // 2))
    project_tile(a1[...], w_ref, acc_ref, slice(na // 2, na))

    @pl.when(r == pl.num_programs(0) - 1)
    def _():
        project_tile(b0[...], w_ref, acc_ref, slice(na, na + nb // 2))
        project_tile(b1[...], w_ref, acc_ref, slice(na + nb // 2, na + nb))
        emit_heads(acc_ref[...], scale_ref, where_ref[4], *outs)


def project_last(where, w, scale, a0, a1, b0, b1, part):
    na, nb, feat = 2 * a0.shape[0], 2 * b0.shape[0], b0.shape[1]
    rows = na + nb
    fixed = lambda x: pl.BlockSpec(x.shape, lambda r, s: (0, 0))
    return pl.pallas_call(
        functools.partial(last_kernel, na, nb),
        grid_spec=pltpu.PrefetchScalarGridSpec(
            num_scalar_prefetch=1,
            grid=(4,),
            in_specs=[
                pl.BlockSpec((3, feat, 256), lambda r, s: (0, s[r], 0)),
                pl.BlockSpec((1, 768), lambda r, s: (0, 0)),
                pl.BlockSpec((na // 2, feat), lambda r, s: (0, r)),
                pl.BlockSpec((na // 2, feat), lambda r, s: (0, r)),
                fixed(b0),
                fixed(b1),
                fixed(part),
            ],
            out_specs=heads_specs(rows),
            scratch_shapes=[pltpu.VMEM((rows, 768), jnp.float32)],
        ),
        out_shape=heads_shape(rows),
        compiler_params=pltpu.CompilerParams(vmem_limit_bytes=40 << 20),
        cost_estimate=pl.CostEstimate(
            flops=2 * rows * 2 * feat * 768, bytes_accessed=w.size * 2, transcendentals=0
        ),
    )(where, w, scale, a0, a1, b0, b1, part)


def attn_kernel(bk, first_block, begin, end, q_ref, qm_ref, *refs):
    kv_refs, o_ref = refs[:-1], refs[-1]
    if not begin:
        state_ref, kv_refs = kv_refs[0], kv_refs[1:]
    rows = q_ref.shape[0]
    q = jnp.concatenate([q_ref[...], qm_ref[...]], axis=1)
    tiles = [(r, j) for r in range(len(kv_refs)) for j in range(kv_refs[r].shape[0] // bk)]
    lane = lax.broadcasted_iota(jnp.int32, (bk, HD), 1)
    inner = lax.broadcasted_iota(jnp.int32, (bk, HD), 0) // BLOCK
    ones = (lane == 0).astype(jnp.float32).astype(jnp.bfloat16)
    per_tile = bk // BLOCK

    def score(i):
        r, j = tiles[i]
        onehot = (lane == inner + (first_block + i * per_tile)).astype(jnp.float32).astype(jnp.bfloat16)
        k = jnp.concatenate([kv_refs[r][j * bk : (j + 1) * bk, :HD], onehot], axis=1)
        return lax.dot_general(q, k, CONTRACT_LAST, preferred_element_type=jnp.float32)

    if begin:
        high = jnp.full((rows, 1), -3e38, jnp.float32)
        acc = jnp.zeros((rows, 2 * HD), jnp.float32)
    else:
        acc = state_ref[...]
        high = acc[:, 2 * HD - 1 :]
    s = score(0)
    for i in range(len(tiles)):
        s_next = score(i + 1) if i + 1 < len(tiles) else None
        new_high = jnp.maximum(high, jnp.max(s, axis=1, keepdims=True))
        p = jnp.exp2(s - new_high).astype(jnp.bfloat16)
        factor = jnp.exp2(high - new_high)
        r, j = tiles[i]
        v = jnp.concatenate([kv_refs[r][j * bk : (j + 1) * bk, HD:], ones], axis=1)
        acc = acc * factor + jnp.dot(p, v, preferred_element_type=jnp.float32)
        high = new_high
        s = s_next
    if end:
        o_ref[...] = (acc[:, :HD] / acc[:, HD : HD + 1]).astype(jnp.bfloat16)
    else:
        o_ref[...] = jnp.where(lax.broadcasted_iota(jnp.int32, acc.shape, 1) == 2 * HD - 1, high, acc)


def attention(q, qm, kvs, first_block, state, end, bk, bq=512):
    rows = q.shape[0]
    keys = sum(kv.shape[0] for kv in kvs)
    begin = state is None
    row_block = lambda n: pl.BlockSpec((bq, n), lambda i: (i, 0))
    return pl.pallas_call(
        functools.partial(attn_kernel, bk, first_block, begin, end),
        grid=(rows // bq,),
        in_specs=[row_block(HD), row_block(HD)]
        + ([] if begin else [row_block(2 * HD)])
        + [pl.BlockSpec(kv.shape, lambda i: (0, 0)) for kv in kvs],
        out_specs=row_block(HD if end else 2 * HD),
        out_shape=jax.ShapeDtypeStruct((rows, HD), jnp.bfloat16)
        if end
        else jax.ShapeDtypeStruct((rows, 2 * HD), jnp.float32),
        compiler_params=pltpu.CompilerParams(vmem_limit_bytes=40 << 20),
        cost_estimate=pl.CostEstimate(
            flops=8 * rows * keys * HD, bytes_accessed=keys * 512, transcendentals=rows * keys
        ),
    )(*([q, qm] if begin else [q, qm, state]), *kvs)


def local(tokens, w_qkv, qkv_scale, block_mask, w_out):
    nu, nb, nt = lax.axis_size("ulysses"), lax.axis_size("blk"), lax.axis_size("tensor")
    u, b, t = lax.axis_index("ulysses"), lax.axis_index("blk"), lax.axis_index("tensor")
    y, core = b // 2, b % 2
    half = tokens.shape[0] // 2
    quarter = half // 2
    pp = lax.ppermute
    offsets = jnp.array(OFFSETS, jnp.int32)

    def direct(value, axis, n):
        return [value] + [pp(value, axis, ring(n, s)) for s in (1, -1, 2)]

    where = jnp.concatenate([(t + offsets) % nt, core[None]])
    w = jnp.transpose(w_qkv, (1, 0, 2))
    scale = qkv_scale * jnp.array([LOG2E / math.sqrt(HD), 1.0, 1.0], jnp.float32)[:, None]
    scale = jnp.repeat(scale.reshape(1, 6), HD, axis=1)

    ny = nb // 2
    groups = (u + offsets) % nu
    cores = jnp.stack([core, 1 - core])

    def block_id(yy, slot, group, odd):
        return (groups[group] * nb + 2 * (yy % ny) + cores[slot]) * 2 + odd

    early = [(g, 0) for g in range(3)]
    late = [(3, 0)] + [(g, 1) for g in range(4)]
    keys = [(y, s) + g for s in (0, 1) for g in late]
    keys += [(yy, s) + g for yy in range(ny) for s in (0, 1) for g in early]
    keys += [(y + o, s) + g for o in (-1, 1) for s in (0, 1) for g in late]
    keys += [(y + 2, s) + g for s in (0, 1) for g in late]
    key_ids = jnp.stack([block_id(*k) for k in keys])
    query_ids = jnp.stack(
        [block_id(y, s, g, odd) for s in (0, 1) for g in range(4) for odd in (0, 1)]
    )
    blocks = jnp.arange(block_mask.shape[1], dtype=jnp.int32)
    key_hot = (key_ids[:, None] == blocks[None, :]).astype(jnp.float32)
    query_hot = (query_ids[:, None] == blocks[None, :]).astype(jnp.float32)
    mask = lax.dynamic_index_in_dim(block_mask, core, 0, keepdims=False).astype(jnp.float32)
    live = query_hot @ mask @ key_hot.T > 0.5
    live = live | (query_ids[:, None] == key_ids[None, :])
    bias = jnp.where(live, 0.0, NEG).astype(jnp.bfloat16)
    bias = jnp.pad(bias, ((0, 0), (0, HD - bias.shape[1])))
    bias = jnp.repeat(bias, BLOCK, axis=0)

    a_own = jnp.concatenate(direct(tokens[:half], "tensor", nt), axis=1)
    b_own = jnp.concatenate(direct(tokens[half:], "ulysses", nu), axis=0)
    a_m = pp(a_own, "ulysses", ring(nu, 1))
    b_m = pp(b_own, "tensor", ring(nt, 1))
    a_p = pp(a_own, "ulysses", ring(nu, -1))
    b_p = pp(b_own, "tensor", ring(nt, -1))
    bh = b_own.shape[0] // 2
    a0 = pp(a_m[:quarter], "ulysses", ring(nu, 1))
    a1 = pp(a_p[quarter:], "ulysses", ring(nu, -1))
    b0 = pp(b_m[:bh], "tensor", ring(nt, 1))
    b1 = pp(b_p[bh:], "tensor", ring(nt, -1))

    q1, kv1, give1 = project_rows(where, w, scale, [a_own, a_m, a_p])
    got1 = pp(give1, "blk", core_swap(nb))
    kv1_all = lax.all_gather(
        jnp.concatenate([kv1, got1[:, HD:]], axis=0),
        "blk",
        axis=0,
        tiled=True,
        axis_index_groups=[list(range(0, nb, 2)), list(range(1, nb, 2))],
    )
    part = project_part(where, w, [b_own, b_m, b_p])
    q2, kv2, give2 = project_last(where, w, scale, a0, a1, b0, b1, part)
    got2 = pp(give2, "blk", core_swap(nb))
    kv2_own = jnp.concatenate([kv2, got2[:, HD:]], axis=0)
    kv2_m = pp(kv2_own, "blk", y_ring(nb, 1))
    kv2_p = pp(kv2_own, "blk", y_ring(nb, -1))
    kh = kv2_own.shape[0] // 2
    kv2_0 = pp(kv2_m[:kh], "blk", y_ring(nb, 1))
    kv2_1 = pp(kv2_p[kh:], "blk", y_ring(nb, -1))

    def in_order(early_q, late_q):
        e = [early_q[i * half : (i + 1) * half] for i in range(3)]
        l = [late_q[i * half : (i + 1) * half] for i in range(5)]
        e.append(l[0])
        return [x for g in range(4) for x in (e[g], l[1 + g])]

    q = jnp.concatenate(in_order(q1, q2) + in_order(got1[:, :HD], got2[:, :HD]), axis=0)

    state = attention(q, bias, [kv2_own], 0, None, False, 640)
    state = attention(q, bias, [kv1_all], 10, state, False, 768)
    state = attention(q, bias, [kv2_m, kv2_p], 34, state, False, 640)
    out = attention(q, bias, [kv2_0, kv2_1], 54, state, True, 640)

    out = out.reshape(2, nu, 2 * half, HD)
    other = pp(out[1], "blk", core_swap(nb))
    mine = out[0]
    first = jnp.where(core == 0, mine, other)
    second = jnp.where(core == 0, other, mine)
    heads = jnp.concatenate([first, second], axis=-1)
    arrived = [heads[0]] + [
        pp(heads[i], "ulysses", ring(nu, OFFSETS[i])) for i in range(1, nu)
    ]
    partial_value = sum(
        jnp.dot(
            v,
            lax.dynamic_index_in_dim(w_out, (u - o) % nu, 0, keepdims=False),
            preferred_element_type=jnp.float32,
        )
        for v, o in zip(arrived, OFFSETS)
    )
    return lax.psum_scatter(
        partial_value.astype(jnp.bfloat16), "tensor", scatter_dimension=1, tiled=True
    )


def solution(mesh):
    return jax.shard_map(
        local,
        mesh=mesh,
        in_specs=(
            P(("ulysses", "blk"), "tensor"),
            P(None, None, ("ulysses", "tensor")),
            P(None, ("ulysses", "tensor")),
            P(("ulysses", "tensor"), None, None),
            P(None, "tensor", None),
        ),
        out_specs=P(("ulysses", "blk"), "tensor"),
        check_vma=False,
    )
```

```python
import functools
import math

import jax
import jax.numpy as jnp
from jax import lax
from jax.experimental import pallas as pl
from jax.experimental.pallas import tpu as pltpu
from jax.sharding import PartitionSpec as P

HD = 128
BLOCK = 128
NEG = -1e30
LOG2E = 1.4426950408889634
OFFSETS = (0, -1, 1, 2)
CONTRACT_LAST = (((1,), (1,)), ((), ()))


def ring(n, step):
    return [(i, (i + step) % n) for i in range(n)]


def y_ring(n, step):
    return [(i, (i + 2 * step) % n) for i in range(n)]


def core_swap(n):
    return [(i, i ^ 1) for i in range(n)]


def emit_heads(acc, scale_ref, core, q_ref, kv_ref, give_ref):
    scaled = (acc * scale_ref[...]).astype(jnp.bfloat16)
    heads = [[scaled[:, c * 256 + h * HD : c * 256 + (h + 1) * HD] for c in range(3)] for h in (0, 1)]
    is_first = core == 0

    @pl.when(is_first)
    def _():
        q_ref[...] = heads[0][0]
        kv_ref[...] = jnp.concatenate(heads[0][1:], axis=1)
        give_ref[...] = jnp.concatenate(heads[1], axis=1)

    @pl.when(jnp.logical_not(is_first))
    def _():
        q_ref[...] = heads[1][0]
        kv_ref[...] = jnp.concatenate(heads[1][1:], axis=1)
        give_ref[...] = jnp.concatenate(heads[0], axis=1)


def heads_shape(rows):
    return [jax.ShapeDtypeStruct((rows, n * HD), jnp.bfloat16) for n in (1, 2, 3)]


def start_weights(where_ref, w_hbm, w_buf, sems):
    feat = w_buf.shape[2]
    copies = []
    for i in range(4):
        rows = pl.ds(pl.multiple_of(where_ref[i] * feat, feat), feat)
        copies.append(pltpu.make_async_copy(w_hbm.at[:, rows, :], w_buf.at[i], sems.at[i]))
        copies[-1].start()
    return copies


def early_kernel(where_ref, w_hbm, scale_ref, *refs):
    a_refs, b_refs = refs[:3], refs[3:6]
    q_ref, kv_ref, give_ref, part_ref, acc_ref, w_buf, sems = refs[6:]
    copies = start_weights(where_ref, w_hbm, w_buf, sems)
    na = a_refs[0].shape[0] // 4
    for i in range(4):
        copies[i].wait()
        rows = pl.ds(pl.multiple_of(where_ref[i] * na, na), na)
        x = [a_ref[rows, :] for a_ref in a_refs]
        if i < 3:
            x.append(b_refs[i][...])
        x = jnp.concatenate(x, axis=0)
        n = x.shape[0]
        for c in range(3):
            cols = slice(c * 256, (c + 1) * 256)
            d = jnp.dot(x, w_buf[i, c], preferred_element_type=jnp.float32)
            acc_ref[:n, cols] = d if i == 0 else acc_ref[:n, cols] + d
    emit_heads(acc_ref[: 3 * na], scale_ref, where_ref[4], q_ref, kv_ref, give_ref)
    part_ref[...] = acc_ref[3 * na :]


def last_kernel(where_ref, w_hbm, scale_ref, a0, a1, b0, b1, part_ref, q_ref, kv_ref, give_ref, acc_ref, xa_ref, w_buf, sems):
    copies = start_weights(where_ref, w_hbm, w_buf, sems)
    ha = a0.shape[0]
    na = ha // 2
    xa_ref[:ha] = a0[...]
    xa_ref[ha:] = a1[...]
    for i in range(4):
        copies[i].wait()
        x = xa_ref[pl.ds(pl.multiple_of(where_ref[i] * na, na), na), :]
        for c in range(3):
            cols = slice(c * 256, (c + 1) * 256)
            if i < 3:
                d = jnp.dot(x, w_buf[i, c], preferred_element_type=jnp.float32)
                acc_ref[:na, cols] = d if i == 0 else acc_ref[:na, cols] + d
            else:
                x_all = jnp.concatenate([x, b0[...], b1[...]], axis=0)
                d = jnp.dot(x_all, w_buf[i, c], preferred_element_type=jnp.float32)
                acc_ref[:na, cols] = acc_ref[:na, cols] + d[:na]
                acc_ref[na:, cols] = part_ref[:, cols] + d[na:]
    emit_heads(acc_ref[...], scale_ref, where_ref[4], q_ref, kv_ref, give_ref)


VM = pl.BlockSpec(memory_space=pltpu.VMEM)
FIXED = [pl.BlockSpec(memory_space=pltpu.SMEM), pl.BlockSpec(memory_space=pltpu.HBM), VM]


def weight_scratch(w):
    return [
        pltpu.VMEM((4, 3, w.shape[1] // 4, w.shape[2]), jnp.bfloat16),
        pltpu.SemaphoreType.DMA((4,)),
    ]


def project_early(where, w, scale, a_parts, b_parts):
    na, nb = a_parts[0].shape[0] // 4, b_parts[0].shape[0]
    return pl.pallas_call(
        early_kernel,
        in_specs=FIXED + [VM] * 6,
        out_specs=[VM] * 4,
        out_shape=heads_shape(3 * na) + [jax.ShapeDtypeStruct((nb, 768), jnp.float32)],
        scratch_shapes=[pltpu.VMEM((3 * na + nb, 768), jnp.float32)] + weight_scratch(w),
        compiler_params=pltpu.CompilerParams(vmem_limit_bytes=52 << 20),
        cost_estimate=pl.CostEstimate(
            flops=2 * 768 * (3 * na * w.shape[1] + nb * w.shape[1] * 3 // 4), bytes_accessed=w.size * 2, transcendentals=0
        ),
    )(where, w, scale, *a_parts, *b_parts)


def project_last(where, w, scale, a0, a1, b0, b1, part):
    na, nb, feat = a0.shape[0] // 2, part.shape[0], a0.shape[1]
    return pl.pallas_call(
        last_kernel,
        in_specs=FIXED + [VM] * 5,
        out_specs=[VM] * 3,
        out_shape=heads_shape(na + nb),
        scratch_shapes=[pltpu.VMEM((na + nb, 768), jnp.float32), pltpu.VMEM((4 * na, feat), jnp.bfloat16)]
        + weight_scratch(w),
        compiler_params=pltpu.CompilerParams(vmem_limit_bytes=56 << 20),
        cost_estimate=pl.CostEstimate(
            flops=2 * 768 * (na * w.shape[1] + nb * feat), bytes_accessed=w.size * 2, transcendentals=0
        ),
    )(where, w, scale, a0, a1, b0, b1, part)


def out_kernel(where_ref, *refs):
    xs, w_ref, o_ref = refs[:4], refs[4], refs[5]
    k = pl.program_id(1)
    for i, x_ref in enumerate(xs):

        @pl.when(k == i)
        def _():
            d = jnp.dot(x_ref[...], w_ref[0], preferred_element_type=jnp.float32)
            if i == 0:
                o_ref[...] = d
            else:
                o_ref[...] += d


def out_project(where, xs, w_out, places):
    rows, cols = xs[0].shape[0], w_out.shape[2] // 4
    n = len(places)
    first = places[0]
    step = places[1] - first if n > 1 else 0
    return pl.pallas_call(
        out_kernel,
        grid_spec=pltpu.PrefetchScalarGridSpec(
            num_scalar_prefetch=1,
            grid=(n, 4),
            in_specs=[pl.BlockSpec(x.shape, lambda r, k, s: (0, 0)) for x in xs]
            + [
                pl.BlockSpec(
                    (1, w_out.shape[1], cols), lambda r, k, s: (s[5 + k], 0, s[first + step * r])
                )
            ],
            out_specs=pl.BlockSpec((rows, cols), lambda r, k, s: (r, 0)),
        ),
        out_shape=jax.ShapeDtypeStruct((n * rows, cols), jnp.float32),
        compiler_params=pltpu.CompilerParams(vmem_limit_bytes=56 << 20),
        cost_estimate=pl.CostEstimate(
            flops=2 * n * rows * 4 * w_out.shape[1] * cols,
            bytes_accessed=n * 8 * w_out.shape[1] * cols,
            transcendentals=0,
        ),
    )(where, *xs, w_out)


def attn_kernel(bk, first_block, begin, end, q_ref, qm_ref, *refs):
    kv_refs, o_ref = refs[:-1], refs[-1]
    if not begin:
        state_ref, kv_refs = kv_refs[0], kv_refs[1:]
    rows = q_ref.shape[0]
    q = jnp.concatenate([q_ref[...], qm_ref[...]], axis=1)
    tiles = [(r, j) for r in range(len(kv_refs)) for j in range(kv_refs[r].shape[0] // bk)]
    lane = lax.broadcasted_iota(jnp.int32, (bk, HD), 1)
    inner = lax.broadcasted_iota(jnp.int32, (bk, HD), 0) // BLOCK
    ones = (lane == 0).astype(jnp.float32).astype(jnp.bfloat16)
    per_tile = bk // BLOCK

    def score(i):
        r, j = tiles[i]
        onehot = (lane == inner + (first_block + i * per_tile)).astype(jnp.float32).astype(jnp.bfloat16)
        k = jnp.concatenate([kv_refs[r][j * bk : (j + 1) * bk, :HD], onehot], axis=1)
        return lax.dot_general(q, k, CONTRACT_LAST, preferred_element_type=jnp.float32)

    if begin:
        high = jnp.full((rows, 1), -3e38, jnp.float32)
        acc = jnp.zeros((rows, 2 * HD), jnp.float32)
    else:
        acc = state_ref[...]
        high = acc[:, 2 * HD - 1 :]
    s = score(0)
    for i in range(len(tiles)):
        s_next = score(i + 1) if i + 1 < len(tiles) else None
        new_high = jnp.maximum(high, jnp.max(s, axis=1, keepdims=True))
        p = jnp.exp2(s - new_high).astype(jnp.bfloat16)
        factor = jnp.exp2(high - new_high)
        r, j = tiles[i]
        v = jnp.concatenate([kv_refs[r][j * bk : (j + 1) * bk, HD:], ones], axis=1)
        acc = acc * factor + jnp.dot(p, v, preferred_element_type=jnp.float32)
        high = new_high
        s = s_next
    if end:
        o_ref[...] = (acc[:, :HD] / acc[:, HD : HD + 1]).astype(jnp.bfloat16)
    else:
        o_ref[...] = jnp.where(lax.broadcasted_iota(jnp.int32, acc.shape, 1) == 2 * HD - 1, high, acc)


def attention(q, qm, kvs, first_block, state, end, bk, bq=512):
    rows = q.shape[0]
    keys = sum(kv.shape[0] for kv in kvs)
    begin = state is None
    row_block = lambda n: pl.BlockSpec((bq, n), lambda i: (i, 0))
    return pl.pallas_call(
        functools.partial(attn_kernel, bk, first_block, begin, end),
        grid=(rows // bq,),
        in_specs=[row_block(HD), row_block(HD)]
        + ([] if begin else [row_block(2 * HD)])
        + [pl.BlockSpec(kv.shape, lambda i: (0, 0)) for kv in kvs],
        out_specs=row_block(HD if end else 2 * HD),
        out_shape=jax.ShapeDtypeStruct((rows, HD), jnp.bfloat16)
        if end
        else jax.ShapeDtypeStruct((rows, 2 * HD), jnp.float32),
        compiler_params=pltpu.CompilerParams(vmem_limit_bytes=24 << 20),
        cost_estimate=pl.CostEstimate(
            flops=8 * rows * keys * HD, bytes_accessed=keys * 512, transcendentals=rows * keys
        ),
    )(*([q, qm] if begin else [q, qm, state]), *kvs)


def local(tokens, w_qkv, qkv_scale, block_mask, w_out):
    nu, nb, nt = lax.axis_size("ulysses"), lax.axis_size("blk"), lax.axis_size("tensor")
    u, b, t = lax.axis_index("ulysses"), lax.axis_index("blk"), lax.axis_index("tensor")
    y, core = b // 2, b % 2
    half = tokens.shape[0] // 2
    quarter = half // 2
    pp = lax.ppermute
    offsets = jnp.array(OFFSETS, jnp.int32)

    def direct(value, axis, n):
        return [value] + [pp(value, axis, ring(n, s)) for s in (1, -1, 2)]

    where = jnp.concatenate([(t + offsets) % nt, core[None], (u - offsets) % nu])
    w = jnp.transpose(w_qkv, (1, 0, 2))
    scale = qkv_scale * jnp.array([LOG2E / math.sqrt(HD), 1.0, 1.0], jnp.float32)[:, None]
    scale = jnp.repeat(scale.reshape(1, 6), HD, axis=1)

    ny = nb // 2
    groups = (u + offsets) % nu
    cores = jnp.stack([core, 1 - core])

    def block_id(yy, slot, group, odd):
        return (groups[group] * nb + 2 * (yy % ny) + cores[slot]) * 2 + odd

    early = [(g, 0) for g in range(3)]
    late = [(3, 0)] + [(g, 1) for g in range(4)]
    keys = [(y, s) + g for s in (0, 1) for g in late]
    keys += [(yy, s) + g for yy in range(ny) for s in (0, 1) for g in early]
    keys += [(y + o, s) + g for o in (-1, 1) for s in (0, 1) for g in late]
    keys += [(y + 2, s) + g for s in (0, 1) for g in late]
    key_ids = jnp.stack([block_id(*k) for k in keys])
    query_ids = jnp.stack(
        [block_id(y, s, g, odd) for s in (0, 1) for g in range(4) for odd in (0, 1)]
    )
    blocks = jnp.arange(block_mask.shape[1], dtype=jnp.int32)
    key_hot = (key_ids[:, None] == blocks[None, :]).astype(jnp.float32)
    query_hot = (query_ids[:, None] == blocks[None, :]).astype(jnp.float32)
    mask = lax.dynamic_index_in_dim(block_mask, core, 0, keepdims=False).astype(jnp.float32)
    live = query_hot @ mask @ key_hot.T > 0.5
    live = live | (query_ids[:, None] == key_ids[None, :])
    bias = jnp.where(live, 0.0, NEG).astype(jnp.bfloat16)
    bias = jnp.pad(bias, ((0, 0), (0, HD - bias.shape[1])))
    bias = jnp.repeat(bias, BLOCK, axis=0)

    a_own = lax.all_gather(tokens[:half], "tensor", axis=0, tiled=True)
    b_own = jnp.concatenate(direct(tokens[half:], "ulysses", nu), axis=0)
    a_m = pp(a_own, "ulysses", ring(nu, 1))
    b_m = pp(b_own, "tensor", ring(nt, 1))
    a_p = pp(a_own, "ulysses", ring(nu, -1))
    b_p = pp(b_own, "tensor", ring(nt, -1))
    ah, bh = a_own.shape[0] // 2, b_own.shape[0] // 2
    a0 = pp(a_m[:ah], "ulysses", ring(nu, 1))
    a1 = pp(a_p[ah:], "ulysses", ring(nu, -1))
    b0 = pp(b_m[:bh], "tensor", ring(nt, 1))
    b1 = pp(b_p[bh:], "tensor", ring(nt, -1))

    q1, kv1, give1, part = project_early(where, w, scale, [a_own, a_m, a_p], [b_own, b_m, b_p])
    got1 = pp(give1, "blk", core_swap(nb))
    kv1_all = lax.all_gather(
        jnp.concatenate([kv1, got1[:, HD:]], axis=0),
        "blk",
        axis=0,
        tiled=True,
        axis_index_groups=[list(range(0, nb, 2)), list(range(1, nb, 2))],
    )
    q2, kv2, give2 = project_last(where, w, scale, a0, a1, b0, b1, part)
    got2 = pp(give2, "blk", core_swap(nb))
    kv2_own = jnp.concatenate([kv2, got2[:, HD:]], axis=0)
    kv2_m = pp(kv2_own, "blk", y_ring(nb, 1))
    kv2_p = pp(kv2_own, "blk", y_ring(nb, -1))
    kh = kv2_own.shape[0] // 2
    kv2_0 = pp(kv2_m[:kh], "blk", y_ring(nb, 1))
    kv2_1 = pp(kv2_p[kh:], "blk", y_ring(nb, -1))

    def in_order(early_q, late_q):
        e = [early_q[i * half : (i + 1) * half] for i in range(3)]
        l = [late_q[i * half : (i + 1) * half] for i in range(5)]
        e.append(l[0])
        return [x for g in range(4) for x in (e[g], l[1 + g])]

    q = jnp.concatenate(in_order(q1, q2) + in_order(got1[:, :HD], got2[:, :HD]), axis=0)

    state = attention(q, bias, [kv2_own], 0, None, False, 640)
    state = attention(q, bias, [kv1_all], 10, state, False, 768)
    state = attention(q, bias, [kv2_m, kv2_p], 34, state, False, 640)
    out = attention(q, bias, [kv2_0, kv2_1], 54, state, True, 640)

    out = out.reshape(2, nu, 2 * half, HD)
    other = pp(out[1], "blk", core_swap(nb))
    mine = out[0]
    first = jnp.where(core == 0, mine, other)
    second = jnp.where(core == 0, other, mine)
    heads = jnp.concatenate([first, second], axis=-1)
    arrived = [heads[0]] + [
        pp(heads[i], "ulysses", ring(nu, OFFSETS[i])) for i in range(1, nu)
    ]
    bf = jnp.bfloat16
    far = out_project(where, arrived, w_out, (3,)).astype(bf)
    rows = far.shape[0]
    hr = rows // 2
    far_m = pp(far[:hr], "tensor", ring(nt, 1))
    far_p = pp(far[hr:], "tensor", ring(nt, -1))
    near = out_project(where, arrived, w_out, (1, 2))
    to_m, to_p = near[:rows], near[rows:]
    to_p = jnp.concatenate([to_p[:hr] + far_m.astype(jnp.float32), to_p[hr:]], axis=0).astype(bf)
    to_m = jnp.concatenate([to_m[:hr], to_m[hr:] + far_p.astype(jnp.float32)], axis=0).astype(bf)
    from_m = pp(to_p, "tensor", ring(nt, 1))
    from_p = pp(to_m, "tensor", ring(nt, -1))
    own = out_project(where, arrived, w_out, (0,))
    return (own + from_m.astype(jnp.float32) + from_p.astype(jnp.float32)).astype(bf)


def solution(mesh):
    return jax.shard_map(
        local,
        mesh=mesh,
        in_specs=(
            P(("ulysses", "blk"), "tensor"),
            P(None, None, ("ulysses", "tensor")),
            P(None, ("ulysses", "tensor")),
            P(("ulysses", "tensor"), None, None),
            P(None, "tensor", None),
        ),
        out_specs=P(("ulysses", "blk"), "tensor"),
        check_vma=False,
    )
```

```python
import functools
import math

import jax
import jax.numpy as jnp
from jax import lax
from jax.experimental import pallas as pl
from jax.experimental.pallas import tpu as pltpu
from jax.sharding import PartitionSpec as P

HD = 128
BLOCK = 128
NEG = -1e30
LOG2E = 1.4426950408889634
OFFSETS = (0, -1, 1, 2)
CONTRACT_LAST = (((1,), (1,)), ((), ()))


def ring(n, step):
    return [(i, (i + step) % n) for i in range(n)]


def y_ring(n, step):
    return [(i, (i + 2 * step) % n) for i in range(n)]


def core_swap(n):
    return [(i, i ^ 1) for i in range(n)]


def emit_heads(acc, scale_ref, core, q_ref, kv_ref, give_ref):
    scaled = (acc * scale_ref[...]).astype(jnp.bfloat16)
    heads = [[scaled[:, c * 256 + h * HD : c * 256 + (h + 1) * HD] for c in range(3)] for h in (0, 1)]
    is_first = core == 0

    @pl.when(is_first)
    def _():
        q_ref[...] = heads[0][0]
        kv_ref[...] = jnp.concatenate(heads[0][1:], axis=1)
        give_ref[...] = jnp.concatenate(heads[1], axis=1)

    @pl.when(jnp.logical_not(is_first))
    def _():
        q_ref[...] = heads[1][0]
        kv_ref[...] = jnp.concatenate(heads[1][1:], axis=1)
        give_ref[...] = jnp.concatenate(heads[0], axis=1)


def heads_shape(rows):
    return [jax.ShapeDtypeStruct((rows, n * HD), jnp.bfloat16) for n in (1, 2, 3)]


def stage_kernel(n_a, b_slices, n_done, has_part, emit_all, where_ref, w_hbm, scale_ref, *refs):
    a_refs, refs = refs[:n_a], refs[n_a:]
    b_refs, refs = refs[: len(b_slices)], refs[len(b_slices) :]
    done_refs, refs = refs[:n_done], refs[n_done:]
    part_refs, refs = refs[:has_part], refs[has_part:]
    outs, (acc_ref, w_buf, sems) = refs[:-3], refs[-3:]
    feat = w_buf.shape[2]
    copies = []
    for i in range(4):
        rows = pl.ds(pl.multiple_of(where_ref[i] * feat, feat), feat)
        copies.append(pltpu.make_async_copy(w_hbm.at[:, rows, :], w_buf.at[i], sems.at[i]))
        copies[-1].start()
    na = sum(r.shape[0] for r in a_refs)
    fresh = not has_part
    for i in range(4):
        copies[i].wait()
        x = [r[:, i * feat : (i + 1) * feat] for r in a_refs]
        x += [r[...] for r, s in zip(b_refs, b_slices) if s == i]
        with_b = len(x) > n_a
        x = jnp.concatenate(x, axis=0) if len(x) > 1 else x[0]
        for c in range(3):
            cols = slice(c * 256, (c + 1) * 256)
            d = jnp.dot(x, w_buf[i, c], preferred_element_type=jnp.float32)
            acc_ref[:na, cols] = d[:na] if i == 0 else acc_ref[:na, cols] + d[:na]
            if with_b:
                first = i == min(b_slices)
                before = None if first and fresh else part_refs[0][:, cols] if first else acc_ref[na:, cols]
                acc_ref[na:, cols] = d[na:] if before is None else before + d[na:]
    if not emit_all and not n_done:
        outs[0][...] = acc_ref[:na]
        outs[1][...] = acc_ref[na:]
        return
    rows = acc_ref[...] if emit_all else acc_ref[:na]
    if n_done:
        rows = jnp.concatenate([done_refs[0][...], rows], axis=0)
    emit_heads(rows, scale_ref, where_ref[4], *outs[:3])
    if not emit_all:
        outs[3][...] = acc_ref[na:]


VM = pl.BlockSpec(memory_space=pltpu.VMEM)
FIXED = [pl.BlockSpec(memory_space=pltpu.SMEM), pl.BlockSpec(memory_space=pltpu.HBM), VM]


def project_stage(where, w, scale, a_parts, b_parts, b_slices, done, part, emit_all, limit):
    feat = w.shape[1] // 4
    na = sum(x.shape[0] for x in a_parts)
    nb = 512 if part is None else part.shape[0]
    f32 = lambda n: jax.ShapeDtypeStruct((n, 768), jnp.float32)
    if emit_all:
        shapes = heads_shape(na + nb)
    elif done is not None:
        shapes = heads_shape(done.shape[0] + na) + [f32(nb)]
    else:
        shapes = [f32(na), f32(nb)]
    extra = [x for x in (done, part) if x is not None]
    return pl.pallas_call(
        functools.partial(
            stage_kernel, len(a_parts), b_slices, int(done is not None), int(part is not None), emit_all
        ),
        in_specs=FIXED + [VM] * (len(a_parts) + len(b_parts) + len(extra)),
        out_specs=[VM] * len(shapes),
        out_shape=shapes,
        scratch_shapes=[
            pltpu.VMEM((na + nb, 768), jnp.float32),
            pltpu.VMEM((4, 3, feat, w.shape[2]), jnp.bfloat16),
            pltpu.SemaphoreType.DMA((4,)),
        ],
        compiler_params=pltpu.CompilerParams(vmem_limit_bytes=limit << 20),
        cost_estimate=pl.CostEstimate(
            flops=2 * 768 * feat * (4 * na + sum(x.shape[0] for x in b_parts)),
            bytes_accessed=w.size * 2,
            transcendentals=0,
        ),
    )(where, w, scale, *a_parts, *b_parts, *extra)


def out_kernel(where_ref, *refs):
    xs, w_ref, o_ref = refs[:4], refs[4], refs[5]
    o_ref[...] = sum(
        jnp.dot(x_ref[...], w_ref[where_ref[5 + i]], preferred_element_type=jnp.float32)
        for i, x_ref in enumerate(xs)
    )


def out_project(where, xs, w_out, places):
    rows, cols = xs[0].shape[0], w_out.shape[2] // 4
    n = len(places)
    first = places[0]
    step = places[1] - first if n > 1 else 0
    return pl.pallas_call(
        out_kernel,
        grid_spec=pltpu.PrefetchScalarGridSpec(
            num_scalar_prefetch=1,
            grid=(n,),
            in_specs=[pl.BlockSpec(x.shape, lambda r, s: (0, 0)) for x in xs]
            + [pl.BlockSpec((4, w_out.shape[1], cols), lambda r, s: (0, 0, s[first + step * r]))],
            out_specs=pl.BlockSpec((rows, cols), lambda r, s: (r, 0)),
        ),
        out_shape=jax.ShapeDtypeStruct((n * rows, cols), jnp.float32),
        compiler_params=pltpu.CompilerParams(vmem_limit_bytes=56 << 20),
        cost_estimate=pl.CostEstimate(
            flops=2 * n * rows * 4 * w_out.shape[1] * cols,
            bytes_accessed=n * 8 * w_out.shape[1] * cols,
            transcendentals=0,
        ),
    )(where, *xs, w_out)


def attn_kernel(bk, first_block, begin, end, q_ref, qm_ref, *refs):
    kv_refs, o_ref = refs[:-1], refs[-1]
    if not begin:
        state_ref, kv_refs = kv_refs[0], kv_refs[1:]
    rows = q_ref.shape[0]
    q = jnp.concatenate([q_ref[...], qm_ref[...]], axis=1)
    tiles = [(r, j) for r in range(len(kv_refs)) for j in range(kv_refs[r].shape[0] // bk)]
    lane = lax.broadcasted_iota(jnp.int32, (bk, HD), 1)
    inner = lax.broadcasted_iota(jnp.int32, (bk, HD), 0) // BLOCK
    ones = (lane == 0).astype(jnp.float32).astype(jnp.bfloat16)
    per_tile = bk // BLOCK

    def score(i):
        r, j = tiles[i]
        onehot = (lane == inner + (first_block + i * per_tile)).astype(jnp.float32).astype(jnp.bfloat16)
        k = jnp.concatenate([kv_refs[r][j * bk : (j + 1) * bk, :HD], onehot], axis=1)
        return lax.dot_general(q, k, CONTRACT_LAST, preferred_element_type=jnp.float32)

    if begin:
        high = jnp.full((rows, 1), -3e38, jnp.float32)
        acc = jnp.zeros((rows, 2 * HD), jnp.float32)
    else:
        acc = state_ref[...]
        high = acc[:, 2 * HD - 1 :]
    s = score(0)
    for i in range(len(tiles)):
        s_next = score(i + 1) if i + 1 < len(tiles) else None
        new_high = jnp.maximum(high, jnp.max(s, axis=1, keepdims=True))
        p = jnp.exp2(s - new_high).astype(jnp.bfloat16)
        factor = jnp.exp2(high - new_high)
        r, j = tiles[i]
        v = jnp.concatenate([kv_refs[r][j * bk : (j + 1) * bk, HD:], ones], axis=1)
        acc = acc * factor + jnp.dot(p, v, preferred_element_type=jnp.float32)
        high = new_high
        s = s_next
    if end:
        o_ref[...] = (acc[:, :HD] / acc[:, HD : HD + 1]).astype(jnp.bfloat16)
    else:
        o_ref[...] = jnp.where(lax.broadcasted_iota(jnp.int32, acc.shape, 1) == 2 * HD - 1, high, acc)


def attention(q, qm, kvs, first_block, state, end, bk, bq=512):
    rows = q.shape[0]
    keys = sum(kv.shape[0] for kv in kvs)
    begin = state is None
    row_block = lambda n: pl.BlockSpec((bq, n), lambda i: (i, 0))
    return pl.pallas_call(
        functools.partial(attn_kernel, bk, first_block, begin, end),
        grid=(rows // bq,),
        in_specs=[row_block(HD), row_block(HD)]
        + ([] if begin else [row_block(2 * HD)])
        + [pl.BlockSpec(kv.shape, lambda i: (0, 0)) for kv in kvs],
        out_specs=row_block(HD if end else 2 * HD),
        out_shape=jax.ShapeDtypeStruct((rows, HD), jnp.bfloat16)
        if end
        else jax.ShapeDtypeStruct((rows, 2 * HD), jnp.float32),
        compiler_params=pltpu.CompilerParams(vmem_limit_bytes=24 << 20),
        cost_estimate=pl.CostEstimate(
            flops=8 * rows * keys * HD, bytes_accessed=keys * 512, transcendentals=rows * keys
        ),
    )(*([q, qm] if begin else [q, qm, state]), *kvs)


def local(tokens, w_qkv, qkv_scale, block_mask, w_out):
    nu, nb, nt = lax.axis_size("ulysses"), lax.axis_size("blk"), lax.axis_size("tensor")
    u, b, t = lax.axis_index("ulysses"), lax.axis_index("blk"), lax.axis_index("tensor")
    y, core = b // 2, b % 2
    half = tokens.shape[0] // 2
    quarter = half // 2
    pp = lax.ppermute
    offsets = jnp.array(OFFSETS, jnp.int32)

    def direct(value, axis, n):
        return [value] + [pp(value, axis, ring(n, s)) for s in (1, -1, 2)]

    where = jnp.concatenate([(t + offsets) % nt, core[None], (u - offsets) % nu])
    w = jnp.transpose(w_qkv, (1, 0, 2))
    scale = qkv_scale * jnp.array([LOG2E / math.sqrt(HD), 1.0, 1.0], jnp.float32)[:, None]
    scale = jnp.repeat(scale.reshape(1, 6), HD, axis=1)

    ny = nb // 2
    groups = (u + offsets) % nu
    cores = jnp.stack([core, 1 - core])

    def block_id(yy, slot, group, odd):
        return (groups[group] * nb + 2 * (yy % ny) + cores[slot]) * 2 + odd

    early = [(g, 0) for g in range(3)]
    late = [(3, 0)] + [(g, 1) for g in range(4)]
    def ring_order(part):
        own = [(y, s) + g for s in (0, 1) for g in part]
        near = [(y + o, s) + g for o in (-1, 1) for s in (0, 1) for g in part]
        far = [(y + 2, s) + g for s in (0, 1) for g in part]
        return own, near, far

    early_ids, late_ids = ring_order(early), ring_order(late)
    keys = sum(early_ids, []) + sum(late_ids, [])
    key_ids = jnp.stack([block_id(*k) for k in keys])
    query_ids = jnp.stack(
        [block_id(y, s, g, odd) for s in (0, 1) for odd in (0, 1) for g in range(4)]
    )
    blocks = jnp.arange(block_mask.shape[1], dtype=jnp.int32)
    key_hot = (key_ids[:, None] == blocks[None, :]).astype(jnp.float32)
    query_hot = (query_ids[:, None] == blocks[None, :]).astype(jnp.float32)
    mask = lax.dynamic_index_in_dim(block_mask, core, 0, keepdims=False).astype(jnp.float32)
    live = query_hot @ mask @ key_hot.T > 0.5
    live = live | (query_ids[:, None] == key_ids[None, :])
    bias = jnp.where(live, 0.0, NEG).astype(jnp.bfloat16)
    bias = jnp.pad(bias, ((0, 0), (0, HD - bias.shape[1])))
    bias = jnp.repeat(bias, BLOCK, axis=0)

    a_own = jnp.concatenate(direct(tokens[:half], "tensor", nt), axis=1)
    b_own = jnp.concatenate(direct(tokens[half:], "ulysses", nu), axis=0)
    a_m = pp(a_own, "ulysses", ring(nu, 1))
    b_m = pp(b_own, "tensor", ring(nt, 1))
    a_p = pp(a_own, "ulysses", ring(nu, -1))
    b_p = pp(b_own, "tensor", ring(nt, -1))
    ah, bh = a_own.shape[0] // 2, b_own.shape[0] // 2
    a0 = pp(a_m[:ah], "ulysses", ring(nu, 1))
    a1 = pp(a_p[ah:], "ulysses", ring(nu, -1))
    b0 = pp(b_m[:bh], "tensor", ring(nt, 1))
    b1 = pp(b_p[bh:], "tensor", ring(nt, -1))

    def swap(kv, give):
        got = pp(give, "blk", core_swap(nb))
        return got[:, :HD], jnp.concatenate([kv, got[:, HD:]], axis=0)

    def near_y(kv):
        return [pp(kv, "blk", y_ring(nb, s)) for s in (1, -1)]

    def far_y(kv_m, kv_p):
        h = kv_m.shape[0] // 2
        return [pp(kv_m[:h], "blk", y_ring(nb, 1)), pp(kv_p[h:], "blk", y_ring(nb, -1))]

    done, part = project_stage(where, w, scale, [a_own], [b_own], (0,), None, None, False, 48)
    q1, kv1, give1, part = project_stage(
        where, w, scale, [a_m, a_p], [b_m, b_p], (1, 2), done, part, False, 46
    )
    q1x, kv1 = swap(kv1, give1)
    kv1_near = near_y(kv1)
    kv1_far = far_y(*kv1_near)
    q2, kv2, give2 = project_stage(where, w, scale, [a0, a1], [b0, b1], (3, 3), None, part, True, 56)
    q2x, kv2 = swap(kv2, give2)
    kv2_near = near_y(kv2)
    kv2_far = far_y(*kv2_near)

    q = jnp.concatenate([q1, q2, q1x, q2x], axis=0)
    state = attention(q, bias, [kv1] + kv1_near, 0, None, False, 768)
    state = attention(q, bias, kv1_far, 18, state, False, 384)
    state = attention(q, bias, [kv2] + kv2_near, 24, state, False, 640)
    out = attention(q, bias, kv2_far, 54, state, True, 640)

    out = out.reshape(2, 2, nu, half, HD)
    other = pp(out[1], "blk", core_swap(nb))
    mine = out[0]
    first = jnp.where(core == 0, mine, other)
    second = jnp.where(core == 0, other, mine)
    heads = jnp.concatenate([first, second], axis=-1)
    heads = [heads[:, g].reshape(2 * half, 2 * HD) for g in range(nu)]
    arrived = [heads[0]] + [
        pp(heads[i], "ulysses", ring(nu, OFFSETS[i])) for i in range(1, nu)
    ]
    bf = jnp.bfloat16
    far = out_project(where, arrived, w_out, (3,)).astype(bf)
    rows = far.shape[0]
    hr = rows // 2
    far_m = pp(far[:hr], "tensor", ring(nt, 1))
    far_p = pp(far[hr:], "tensor", ring(nt, -1))
    near = out_project(where, arrived, w_out, (1, 2))
    to_m, to_p = near[:rows], near[rows:]
    to_p = jnp.concatenate([to_p[:hr] + far_m.astype(jnp.float32), to_p[hr:]], axis=0).astype(bf)
    to_m = jnp.concatenate([to_m[:hr], to_m[hr:] + far_p.astype(jnp.float32)], axis=0).astype(bf)
    from_m = pp(to_p, "tensor", ring(nt, 1))
    from_p = pp(to_m, "tensor", ring(nt, -1))
    own = out_project(where, arrived, w_out, (0,))
    return (own + from_m.astype(jnp.float32) + from_p.astype(jnp.float32)).astype(bf)


def solution(mesh):
    return jax.shard_map(
        local,
        mesh=mesh,
        in_specs=(
            P(("ulysses", "blk"), "tensor"),
            P(None, None, ("ulysses", "tensor")),
            P(None, ("ulysses", "tensor")),
            P(("ulysses", "tensor"), None, None),
            P(None, "tensor", None),
        ),
        out_specs=P(("ulysses", "blk"), "tensor"),
        check_vma=False,
    )
```

```python
import functools
import math

import jax
import jax.numpy as jnp
from jax import lax
from jax.experimental import pallas as pl
from jax.experimental.pallas import tpu as pltpu
from jax.sharding import PartitionSpec as P

HD = 128
BLOCK = 128
NEG = -1e30
LOG2E = 1.4426950408889634
OFFSETS = (0, -1, 1, 2)
CONTRACT_LAST = (((1,), (1,)), ((), ()))


def ring(n, step):
    return [(i, (i + step) % n) for i in range(n)]


def y_ring(n, step):
    return [(i, (i + 2 * step) % n) for i in range(n)]


def core_swap(n):
    return [(i, i ^ 1) for i in range(n)]


def emit_heads(acc, scale_ref, core, q_ref, kv_ref, give_ref):
    scaled = (acc * scale_ref[...]).astype(jnp.bfloat16)
    heads = [[scaled[:, c * 256 + h * HD : c * 256 + (h + 1) * HD] for c in range(3)] for h in (0, 1)]
    is_first = core == 0

    @pl.when(is_first)
    def _():
        q_ref[...] = heads[0][0]
        kv_ref[...] = jnp.concatenate(heads[0][1:], axis=1)
        give_ref[...] = jnp.concatenate(heads[1], axis=1)

    @pl.when(jnp.logical_not(is_first))
    def _():
        q_ref[...] = heads[1][0]
        kv_ref[...] = jnp.concatenate(heads[1][1:], axis=1)
        give_ref[...] = jnp.concatenate(heads[0], axis=1)


def heads_shape(rows):
    return [jax.ShapeDtypeStruct((rows, n * HD), jnp.bfloat16) for n in (1, 2, 3)]


def stage_kernel(n_a, b_slices, n_done, has_part, emit_all, where_ref, w_hbm, scale_ref, *refs):
    a_refs, refs = refs[:n_a], refs[n_a:]
    b_refs, refs = refs[: len(b_slices)], refs[len(b_slices) :]
    done_refs, refs = refs[:n_done], refs[n_done:]
    part_refs, refs = refs[:has_part], refs[has_part:]
    outs, (acc_ref, w_buf, sems) = refs[:-3], refs[-3:]
    feat = w_buf.shape[2]
    copies = []
    for i in range(4):
        rows = pl.ds(pl.multiple_of(where_ref[i] * feat, feat), feat)
        copies.append(pltpu.make_async_copy(w_hbm.at[:, rows, :], w_buf.at[i], sems.at[i]))
        copies[-1].start()
    na = sum(r.shape[0] for r in a_refs)
    fresh = not has_part
    for i in range(4):
        copies[i].wait()
        x = [r[:, i * feat : (i + 1) * feat] for r in a_refs]
        x += [r[...] for r, s in zip(b_refs, b_slices) if s == i]
        with_b = len(x) > n_a
        x = jnp.concatenate(x, axis=0) if len(x) > 1 else x[0]
        for c in range(3):
            cols = slice(c * 256, (c + 1) * 256)
            d = jnp.dot(x, w_buf[i, c], preferred_element_type=jnp.float32)
            acc_ref[:na, cols] = d[:na] if i == 0 else acc_ref[:na, cols] + d[:na]
            if with_b:
                first = i == min(b_slices)
                before = None if first and fresh else part_refs[0][:, cols] if first else acc_ref[na:, cols]
                acc_ref[na:, cols] = d[na:] if before is None else before + d[na:]
    if not emit_all and not n_done:
        outs[0][...] = acc_ref[:na]
        outs[1][...] = acc_ref[na:]
        return
    rows = acc_ref[...] if emit_all else acc_ref[:na]
    if n_done:
        rows = jnp.concatenate([done_refs[0][...], rows], axis=0)
    emit_heads(rows, scale_ref, where_ref[4], *outs[:3])
    if not emit_all:
        outs[3][...] = acc_ref[na:]


VM = pl.BlockSpec(memory_space=pltpu.VMEM)
FIXED = [pl.BlockSpec(memory_space=pltpu.SMEM), pl.BlockSpec(memory_space=pltpu.HBM), VM]


def project_stage(where, w, scale, a_parts, b_parts, b_slices, done, part, emit_all, limit):
    feat = w.shape[1] // 4
    na = sum(x.shape[0] for x in a_parts)
    nb = 512 if part is None else part.shape[0]
    f32 = lambda n: jax.ShapeDtypeStruct((n, 768), jnp.float32)
    if emit_all:
        shapes = heads_shape(na + nb)
    elif done is not None:
        shapes = heads_shape(done.shape[0] + na) + [f32(nb)]
    else:
        shapes = [f32(na), f32(nb)]
    extra = [x for x in (done, part) if x is not None]
    return pl.pallas_call(
        functools.partial(
            stage_kernel, len(a_parts), b_slices, int(done is not None), int(part is not None), emit_all
        ),
        in_specs=FIXED + [VM] * (len(a_parts) + len(b_parts) + len(extra)),
        out_specs=[VM] * len(shapes),
        out_shape=shapes,
        scratch_shapes=[
            pltpu.VMEM((na + nb, 768), jnp.float32),
            pltpu.VMEM((4, 3, feat, w.shape[2]), jnp.bfloat16),
            pltpu.SemaphoreType.DMA((4,)),
        ],
        compiler_params=pltpu.CompilerParams(vmem_limit_bytes=limit << 20),
        cost_estimate=pl.CostEstimate(
            flops=2 * 768 * feat * (4 * na + sum(x.shape[0] for x in b_parts)),
            bytes_accessed=w.size * 2,
            transcendentals=0,
        ),
    )(where, w, scale, *a_parts, *b_parts, *extra)


def out_kernel(where_ref, *refs):
    xs, w_ref, o_ref = refs[:4], refs[4], refs[5]
    o_ref[...] = sum(
        jnp.dot(x_ref[...], w_ref[where_ref[5 + i]], preferred_element_type=jnp.float32)
        for i, x_ref in enumerate(xs)
    )


def out_project(where, xs, w_out, places):
    rows, cols = xs[0].shape[0], w_out.shape[2] // 4
    n = len(places)
    first = places[0]
    step = places[1] - first if n > 1 else 0
    return pl.pallas_call(
        out_kernel,
        grid_spec=pltpu.PrefetchScalarGridSpec(
            num_scalar_prefetch=1,
            grid=(n,),
            in_specs=[pl.BlockSpec(x.shape, lambda r, s: (0, 0)) for x in xs]
            + [pl.BlockSpec((4, w_out.shape[1], cols), lambda r, s: (0, 0, s[first + step * r]))],
            out_specs=pl.BlockSpec((rows, cols), lambda r, s: (r, 0)),
        ),
        out_shape=jax.ShapeDtypeStruct((n * rows, cols), jnp.float32),
        compiler_params=pltpu.CompilerParams(vmem_limit_bytes=56 << 20),
        cost_estimate=pl.CostEstimate(
            flops=2 * n * rows * 4 * w_out.shape[1] * cols,
            bytes_accessed=n * 8 * w_out.shape[1] * cols,
            transcendentals=0,
        ),
    )(where, *xs, w_out)


def attn_kernel(sizes, first_block, begin, end, q_ref, qm_ref, *refs):
    if not begin:
        state_refs, refs = refs[:3], refs[3:]
    kv_refs, outs = refs[: len(sizes)], refs[len(sizes) :]
    rows = q_ref.shape[0]
    q = jnp.concatenate([q_ref[...], qm_ref[...]], axis=1)
    tiles = []
    for kv_ref, bk in zip(kv_refs, sizes):
        for j in range(0, kv_ref.shape[0], bk):
            tiles.append((kv_ref, slice(j, j + bk), bk, first_block))
            first_block += bk // BLOCK

    def score(tile):
        kv_ref, at, bk, block = tile
        lane = lax.broadcasted_iota(jnp.int32, (bk, HD), 1)
        inner = lax.broadcasted_iota(jnp.int32, (bk, HD), 0) // BLOCK
        onehot = (lane == inner + block).astype(jnp.float32).astype(jnp.bfloat16)
        k = jnp.concatenate([kv_ref[at, :HD], onehot], axis=1)
        return lax.dot_general(q, k, CONTRACT_LAST, preferred_element_type=jnp.float32)

    s = score(tiles[0])
    for i, (kv_ref, at, bk, _) in enumerate(tiles):
        s_next = score(tiles[i + 1]) if i + 1 < len(tiles) else None
        top = jnp.max(s, axis=1, keepdims=True)
        v = jnp.concatenate([kv_ref[at, HD:], jnp.ones((bk, HD), jnp.bfloat16)], axis=1)
        fresh = begin and i == 0
        if fresh:
            high = jnp.broadcast_to(top, (rows, HD))
        else:
            if i == 0:
                old = state_refs[2][...]
                acc = jnp.concatenate([state_refs[0][...], state_refs[1][...]], axis=1)
            else:
                old = high
            high = jnp.maximum(old, top)
        p = jnp.exp2(s - jnp.concatenate([high] * (bk // HD), axis=1)).astype(jnp.bfloat16)
        d = jnp.dot(p, v, preferred_element_type=jnp.float32)
        if fresh:
            acc = d
        else:
            factor = jnp.exp2(old - high)
            acc = acc * jnp.concatenate([factor, factor], axis=1) + d
        s = s_next
    if end:
        outs[0][...] = (acc[:, :HD] / acc[:, HD:]).astype(jnp.bfloat16)
    else:
        outs[0][...] = acc[:, :HD]
        outs[1][...] = acc[:, HD:]
        outs[2][...] = high


def attention(q, qm, kvs, sizes, first_block, state, end, bq=1024):
    rows = q.shape[0]
    keys = sum(kv.shape[0] for kv in kvs)
    begin = state is None
    block = pl.BlockSpec((bq, HD), lambda i: (i, 0))
    f32 = jax.ShapeDtypeStruct((rows, HD), jnp.float32)
    return pl.pallas_call(
        functools.partial(attn_kernel, sizes, first_block, begin, end),
        grid=(rows // bq,),
        in_specs=[block] * (2 if begin else 5)
        + [pl.BlockSpec(kv.shape, lambda i: (0, 0)) for kv in kvs],
        out_specs=block if end else [block] * 3,
        out_shape=jax.ShapeDtypeStruct((rows, HD), jnp.bfloat16) if end else [f32] * 3,
        compiler_params=pltpu.CompilerParams(vmem_limit_bytes=28 << 20),
        cost_estimate=pl.CostEstimate(
            flops=8 * rows * keys * HD, bytes_accessed=keys * 512, transcendentals=rows * keys
        ),
    )(q, qm, *([] if begin else state), *kvs)


def local(tokens, w_qkv, qkv_scale, block_mask, w_out):
    nu, nb, nt = lax.axis_size("ulysses"), lax.axis_size("blk"), lax.axis_size("tensor")
    u, b, t = lax.axis_index("ulysses"), lax.axis_index("blk"), lax.axis_index("tensor")
    y, core = b // 2, b % 2
    half = tokens.shape[0] // 2
    quarter = half // 2
    pp = lax.ppermute
    offsets = jnp.array(OFFSETS, jnp.int32)

    def direct(value, axis, n):
        return [value] + [pp(value, axis, ring(n, s)) for s in (1, -1, 2)]

    where = jnp.concatenate([(t + offsets) % nt, core[None], (u - offsets) % nu])
    w = jnp.transpose(w_qkv, (1, 0, 2))
    scale = qkv_scale * jnp.array([LOG2E / math.sqrt(HD), 1.0, 1.0], jnp.float32)[:, None]
    scale = jnp.repeat(scale.reshape(1, 6), HD, axis=1)

    ny = nb // 2
    groups = (u + offsets) % nu
    cores = jnp.stack([core, 1 - core])

    def block_id(yy, slot, group, odd):
        return (groups[group] * nb + 2 * (yy % ny) + cores[slot]) * 2 + odd

    early = [(g, 0) for g in range(3)]
    late = [(3, 0)] + [(g, 1) for g in range(4)]
    def ring_order(part):
        own = [(y, s) + g for s in (0, 1) for g in part]
        near = [(y + o, s) + g for o in (-1, 1) for s in (0, 1) for g in part]
        far = [(y + 2, s) + g for s in (0, 1) for g in part]
        return own, near, far

    early_ids, late_ids = ring_order(early), ring_order(late)
    keys = sum(early_ids, []) + sum(late_ids, [])
    key_ids = jnp.stack([block_id(*k) for k in keys])
    query_ids = jnp.stack(
        [block_id(y, s, g, odd) for s in (0, 1) for odd in (0, 1) for g in range(4)]
    )
    blocks = jnp.arange(block_mask.shape[1], dtype=jnp.int32)
    key_hot = (key_ids[:, None] == blocks[None, :]).astype(jnp.float32)
    query_hot = (query_ids[:, None] == blocks[None, :]).astype(jnp.float32)
    mask = lax.dynamic_index_in_dim(block_mask, core, 0, keepdims=False).astype(jnp.float32)
    live = query_hot @ mask @ key_hot.T > 0.5
    live = live | (query_ids[:, None] == key_ids[None, :])
    bias = jnp.where(live, 0.0, NEG).astype(jnp.bfloat16)
    bias = jnp.pad(bias, ((0, 0), (0, HD - bias.shape[1])))
    bias = jnp.repeat(bias, BLOCK, axis=0)

    a_own = jnp.concatenate(direct(tokens[:half], "tensor", nt), axis=1)
    b_own = jnp.concatenate(direct(tokens[half:], "ulysses", nu), axis=0)
    a_m = pp(a_own, "ulysses", ring(nu, 1))
    b_m = pp(b_own, "tensor", ring(nt, 1))
    a_p = pp(a_own, "ulysses", ring(nu, -1))
    b_p = pp(b_own, "tensor", ring(nt, -1))
    ah, bh = a_own.shape[0] // 2, b_own.shape[0] // 2
    a0 = pp(a_m[:ah], "ulysses", ring(nu, 1))
    a1 = pp(a_p[ah:], "ulysses", ring(nu, -1))
    b0 = pp(b_m[:bh], "tensor", ring(nt, 1))
    b1 = pp(b_p[bh:], "tensor", ring(nt, -1))

    def swap(kv, give):
        got = pp(give, "blk", core_swap(nb))
        return got[:, :HD], jnp.concatenate([kv, got[:, HD:]], axis=0)

    def near_y(kv):
        return [pp(kv, "blk", y_ring(nb, s)) for s in (1, -1)]

    def far_y(kv_m, kv_p):
        h = kv_m.shape[0] // 2
        return [pp(kv_m[:h], "blk", y_ring(nb, 1)), pp(kv_p[h:], "blk", y_ring(nb, -1))]

    hold = lax.optimization_barrier
    done, part = project_stage(where, w, scale, [a_own], [b_own], (0,), None, None, False, 48)
    done, bias = hold((done, bias))
    q1, kv1, give1, part = project_stage(
        where, w, scale, [a_m, a_p], [b_m, b_p], (1, 2), done, part, False, 46
    )
    q1x, kv1 = swap(kv1, give1)
    kv1_near = near_y(kv1)
    q2, kv2, give2 = project_stage(where, w, scale, [a0, a1], [b0, b1], (3, 3), None, part, True, 56)
    give2, kv1_near = hold((give2, kv1_near))
    q2x, kv2 = swap(kv2, give2)
    kv1_far = far_y(*kv1_near)
    kv2_near = near_y(kv2)
    kv2_far = far_y(*kv2_near)

    q = jnp.concatenate([q1, q2, q1x, q2x], axis=0)
    state = attention(q, bias, [kv1] + kv1_near, (768,) * 3, 0, None, False)
    state = attention(q, bias, kv1_far + [kv2], (384, 384, 640), 18, state, False)
    state = attention(q, bias, kv2_near, (640, 640), 34, state, False)
    out = attention(q, bias, kv2_far, (640, 640), 54, state, True)

    out = out.reshape(2, 2, nu, half, HD)
    other = pp(out[1], "blk", core_swap(nb))
    mine = out[0]
    first = jnp.where(core == 0, mine, other)
    second = jnp.where(core == 0, other, mine)
    heads = jnp.concatenate([first, second], axis=-1)
    heads = [heads[:, g].reshape(2 * half, 2 * HD) for g in range(nu)]
    arrived = [heads[0]] + [
        pp(heads[i], "ulysses", ring(nu, OFFSETS[i])) for i in range(1, nu)
    ]
    bf = jnp.bfloat16
    far = out_project(where, arrived, w_out, (3,)).astype(bf)
    rows = far.shape[0]
    hr = rows // 2
    far_m = pp(far[:hr], "tensor", ring(nt, 1))
    far_p = pp(far[hr:], "tensor", ring(nt, -1))
    near = out_project(where, arrived, w_out, (1, 2))
    to_m, to_p = near[:rows], near[rows:]
    to_p = jnp.concatenate([to_p[:hr] + far_m.astype(jnp.float32), to_p[hr:]], axis=0).astype(bf)
    to_m = jnp.concatenate([to_m[:hr], to_m[hr:] + far_p.astype(jnp.float32)], axis=0).astype(bf)
    from_m = pp(to_p, "tensor", ring(nt, 1))
    from_p = pp(to_m, "tensor", ring(nt, -1))
    own = out_project(where, arrived, w_out, (0,))
    return (own + from_m.astype(jnp.float32) + from_p.astype(jnp.float32)).astype(bf)


def solution(mesh):
    return jax.shard_map(
        local,
        mesh=mesh,
        in_specs=(
            P(("ulysses", "blk"), "tensor"),
            P(None, None, ("ulysses", "tensor")),
            P(None, ("ulysses", "tensor")),
            P(("ulysses", "tensor"), None, None),
            P(None, "tensor", None),
        ),
        out_specs=P(("ulysses", "blk"), "tensor"),
        check_vma=False,
    )
```

```python
import functools
import math

import jax
import jax.numpy as jnp
from jax import lax
from jax.experimental import pallas as pl
from jax.experimental.pallas import tpu as pltpu
from jax.sharding import PartitionSpec as P

HD = 128
BLOCK = 128
NEG = -1e30
LOG2E = 1.4426950408889634
OFFSETS = (0, -1, 1, 2)
CONTRACT_LAST = (((1,), (1,)), ((), ()))


def ring(n, step):
    return [(i, (i + step) % n) for i in range(n)]


def y_ring(n, step):
    return [(i, (i + 2 * step) % n) for i in range(n)]


def core_swap(n):
    return [(i, i ^ 1) for i in range(n)]


def emit_heads(acc, scale_ref, core, q_ref, kv_ref, give_ref):
    scaled = (acc * scale_ref[...]).astype(jnp.bfloat16)
    heads = [[scaled[:, c * 256 + h * HD : c * 256 + (h + 1) * HD] for c in range(3)] for h in (0, 1)]
    is_first = core == 0

    @pl.when(is_first)
    def _():
        q_ref[...] = heads[0][0]
        kv_ref[...] = jnp.concatenate(heads[0][1:], axis=1)
        give_ref[...] = jnp.concatenate(heads[1], axis=1)

    @pl.when(jnp.logical_not(is_first))
    def _():
        q_ref[...] = heads[1][0]
        kv_ref[...] = jnp.concatenate(heads[1][1:], axis=1)
        give_ref[...] = jnp.concatenate(heads[0], axis=1)


def heads_shape(rows):
    return [jax.ShapeDtypeStruct((rows, n * HD), jnp.bfloat16) for n in (1, 2, 3)]


def load_kernel(pick, where_ref, hbm, o_ref, sems):
    copies = []
    for i in range(o_ref.shape[0]):
        copies.append(pltpu.make_async_copy(pick(hbm, where_ref[i]), o_ref.at[i], sems.at[i]))
        copies[-1].start()
    for copy in copies:
        copy.wait()


def load(where, w, shape, pick, limit):
    return pl.pallas_call(
        functools.partial(load_kernel, pick),
        in_specs=[pl.BlockSpec(memory_space=pltpu.SMEM), pl.BlockSpec(memory_space=pltpu.HBM)],
        out_specs=VM,
        out_shape=jax.ShapeDtypeStruct((4,) + shape, w.dtype),
        scratch_shapes=[pltpu.SemaphoreType.DMA((4,))],
        compiler_params=pltpu.CompilerParams(vmem_limit_bytes=limit << 20),
        cost_estimate=pl.CostEstimate(flops=0, bytes_accessed=w.size * 4, transcendentals=0),
    )(where, w)


def stage_kernel(n_a, b_slices, n_done, has_part, emit_all, where_ref, w_ref, scale_ref, *refs):
    a_refs, refs = refs[:n_a], refs[n_a:]
    b_refs, refs = refs[: len(b_slices)], refs[len(b_slices) :]
    done_refs, refs = refs[:n_done], refs[n_done:]
    part_refs, refs = refs[:has_part], refs[has_part:]
    outs, acc_ref = refs[:-1], refs[-1]
    feat = w_ref.shape[2]
    na = sum(r.shape[0] for r in a_refs)
    fresh = not has_part
    for i in range(4):
        x = [r[:, i * feat : (i + 1) * feat] for r in a_refs]
        x += [r[...] for r, s in zip(b_refs, b_slices) if s == i]
        with_b = len(x) > n_a
        x = jnp.concatenate(x, axis=0) if len(x) > 1 else x[0]
        for c in range(3):
            cols = slice(c * 256, (c + 1) * 256)
            d = jnp.dot(x, w_ref[i, c], preferred_element_type=jnp.float32)
            acc_ref[:na, cols] = d[:na] if i == 0 else acc_ref[:na, cols] + d[:na]
            if with_b:
                first = i == min(b_slices)
                before = None if first and fresh else part_refs[0][:, cols] if first else acc_ref[na:, cols]
                acc_ref[na:, cols] = d[na:] if before is None else before + d[na:]
    if not emit_all and not n_done:
        outs[0][...] = acc_ref[:na]
        outs[1][...] = acc_ref[na:]
        return
    rows = acc_ref[...] if emit_all else acc_ref[:na]
    if n_done:
        rows = jnp.concatenate([done_refs[0][...], rows], axis=0)
    emit_heads(rows, scale_ref, where_ref[4], *outs[:3])
    if not emit_all:
        outs[3][...] = acc_ref[na:]


VM = pl.BlockSpec(memory_space=pltpu.VMEM)
FIXED = [pl.BlockSpec(memory_space=pltpu.SMEM), VM, VM]


def project_stage(where, w, scale, a_parts, b_parts, b_slices, done, part, emit_all):
    feat = w.shape[2]
    na = sum(x.shape[0] for x in a_parts)
    nb = 512 if part is None else part.shape[0]
    f32 = lambda n: jax.ShapeDtypeStruct((n, 768), jnp.float32)
    if emit_all:
        shapes = heads_shape(na + nb)
    elif done is not None:
        shapes = heads_shape(done.shape[0] + na) + [f32(nb)]
    else:
        shapes = [f32(na), f32(nb)]
    extra = [x for x in (done, part) if x is not None]
    return pl.pallas_call(
        functools.partial(
            stage_kernel, len(a_parts), b_slices, int(done is not None), int(part is not None), emit_all
        ),
        in_specs=FIXED + [VM] * (len(a_parts) + len(b_parts) + len(extra)),
        out_specs=[VM] * len(shapes),
        out_shape=shapes,
        scratch_shapes=[pltpu.VMEM((na + nb, 768), jnp.float32)],
        compiler_params=pltpu.CompilerParams(vmem_limit_bytes=16 << 20),
        cost_estimate=pl.CostEstimate(
            flops=2 * 768 * feat * (4 * na + sum(x.shape[0] for x in b_parts)),
            bytes_accessed=w.size * 2,
            transcendentals=0,
        ),
    )(where, w, scale, *a_parts, *b_parts, *extra)


def out_kernel(places, where_ref, *refs):
    xs, w_ref, outs = refs[:4], refs[4], refs[5:]
    per_place = len(outs) // len(places)
    for n, place in enumerate(places):
        d = sum(
            jnp.dot(x_ref[...], w_ref[place, where_ref[5 + i]], preferred_element_type=jnp.float32)
            for i, x_ref in enumerate(xs)
        )
        at = 0
        for o_ref in outs[n * per_place : (n + 1) * per_place]:
            o_ref[...] = d[at : at + o_ref.shape[0]].astype(o_ref.dtype)
            at += o_ref.shape[0]


def out_project(where, xs, w, places, dtype, pieces):
    rows, cols = xs[0].shape[0], w.shape[3]
    n = len(places) * pieces
    return pl.pallas_call(
        functools.partial(out_kernel, places),
        in_specs=[pl.BlockSpec(memory_space=pltpu.SMEM)] + [VM] * 5,
        out_specs=[VM] * n,
        out_shape=[jax.ShapeDtypeStruct((rows // pieces, cols), dtype)] * n,
        compiler_params=pltpu.CompilerParams(vmem_limit_bytes=16 << 20),
        cost_estimate=pl.CostEstimate(
            flops=2 * len(places) * rows * 1024 * cols, bytes_accessed=n * 4 * rows * cols, transcendentals=0
        ),
    )(where, *xs, w)


def attn_kernel(sizes, first_block, begin, end, q_ref, qm_ref, *refs):
    if not begin:
        state_refs, refs = refs[:3], refs[3:]
    kv_refs, outs = refs[: len(sizes)], refs[len(sizes) :]
    rows = q_ref.shape[0]
    q = jnp.concatenate([q_ref[...], qm_ref[...]], axis=1)
    tiles = []
    for kv_ref, bk in zip(kv_refs, sizes):
        for j in range(0, kv_ref.shape[0], bk):
            tiles.append((kv_ref, slice(j, j + bk), bk, first_block))
            first_block += bk // BLOCK

    def score(tile):
        kv_ref, at, bk, block = tile
        lane = lax.broadcasted_iota(jnp.int32, (bk, HD), 1)
        inner = lax.broadcasted_iota(jnp.int32, (bk, HD), 0) // BLOCK
        onehot = (lane == inner + block).astype(jnp.float32).astype(jnp.bfloat16)
        k = jnp.concatenate([kv_ref[at, :HD], onehot], axis=1)
        return lax.dot_general(q, k, CONTRACT_LAST, preferred_element_type=jnp.float32)

    s = score(tiles[0])
    for i, (kv_ref, at, bk, _) in enumerate(tiles):
        s_next = score(tiles[i + 1]) if i + 1 < len(tiles) else None
        top = jnp.max(s, axis=1, keepdims=True)
        v = jnp.concatenate([kv_ref[at, HD:], jnp.ones((bk, HD), jnp.bfloat16)], axis=1)
        fresh = begin and i == 0
        if fresh:
            high = jnp.broadcast_to(top, (rows, HD))
        else:
            if i == 0:
                old = state_refs[2][...]
                acc = jnp.concatenate([state_refs[0][...], state_refs[1][...]], axis=1)
            else:
                old = high
            high = jnp.maximum(old, top)
        p = jnp.exp2(s - jnp.concatenate([high] * (bk // HD), axis=1)).astype(jnp.bfloat16)
        d = jnp.dot(p, v, preferred_element_type=jnp.float32)
        if fresh:
            acc = d
        else:
            factor = jnp.exp2(old - high)
            acc = acc * jnp.concatenate([factor, factor], axis=1) + d
        s = s_next
    if end:
        outs[0][...] = (acc[:, :HD] / acc[:, HD:]).astype(jnp.bfloat16)
    else:
        outs[0][...] = acc[:, :HD]
        outs[1][...] = acc[:, HD:]
        outs[2][...] = high


def attention(q, qm, kvs, sizes, first_block, state, end, bq=1024):
    rows = q.shape[0]
    keys = sum(kv.shape[0] for kv in kvs)
    begin = state is None
    block = pl.BlockSpec((bq, HD), lambda i: (i, 0))
    f32 = jax.ShapeDtypeStruct((rows, HD), jnp.float32)
    return pl.pallas_call(
        functools.partial(attn_kernel, sizes, first_block, begin, end),
        grid=(rows // bq,),
        in_specs=[block] * (2 if begin else 5)
        + [pl.BlockSpec(kv.shape, lambda i: (0, 0)) for kv in kvs],
        out_specs=block if end else [block] * 3,
        out_shape=jax.ShapeDtypeStruct((rows, HD), jnp.bfloat16) if end else [f32] * 3,
        compiler_params=pltpu.CompilerParams(vmem_limit_bytes=28 << 20),
        cost_estimate=pl.CostEstimate(
            flops=8 * rows * keys * HD, bytes_accessed=keys * 512, transcendentals=rows * keys
        ),
    )(q, qm, *([] if begin else state), *kvs)


def local(tokens, w_qkv, qkv_scale, block_mask, w_out):
    nu, nb, nt = lax.axis_size("ulysses"), lax.axis_size("blk"), lax.axis_size("tensor")
    u, b, t = lax.axis_index("ulysses"), lax.axis_index("blk"), lax.axis_index("tensor")
    y, core = b // 2, b % 2
    half = tokens.shape[0] // 2
    quarter = half // 2
    pp = lax.ppermute
    offsets = jnp.array(OFFSETS, jnp.int32)

    def direct(value, axis, n):
        return [value] + [pp(value, axis, ring(n, s)) for s in (1, -1, 2)]

    where = jnp.concatenate([(t + offsets) % nt, core[None], (u - offsets) % nu])
    feat = tokens.shape[1]

    def at_rows(ref, i):
        return ref.at[:, pl.ds(pl.multiple_of(i * feat, feat), feat), :]

    def at_cols(ref, i):
        return ref.at[:, :, pl.ds(pl.multiple_of(i * feat, feat), feat)]

    hold = lax.optimization_barrier
    w = load(where, jnp.transpose(w_qkv, (1, 0, 2)), (3, feat, w_qkv.shape[2]), at_rows, 46)
    w_o = load(where, w_out, w_out.shape[:2] + (feat,), at_cols, 34)
    scale = qkv_scale * jnp.array([LOG2E / math.sqrt(HD), 1.0, 1.0], jnp.float32)[:, None]
    scale = jnp.repeat(scale.reshape(1, 6), HD, axis=1)

    ny = nb // 2
    groups = (u + offsets) % nu
    cores = jnp.stack([core, 1 - core])

    def block_id(yy, slot, group, odd):
        return (groups[group] * nb + 2 * (yy % ny) + cores[slot]) * 2 + odd

    early = [(g, 0) for g in range(3)]
    late = [(3, 0)] + [(g, 1) for g in range(4)]
    def ring_order(part):
        own = [(y, s) + g for s in (0, 1) for g in part]
        near = [(y + o, s) + g for o in (-1, 1) for s in (0, 1) for g in part]
        far = [(y + 2, s) + g for s in (0, 1) for g in part]
        return own, near, far

    early_ids, late_ids = ring_order(early), ring_order(late)
    keys = sum(early_ids, []) + sum(late_ids, [])
    key_ids = jnp.stack([block_id(*k) for k in keys])
    query_ids = jnp.stack(
        [block_id(y, s, g, odd) for s in (0, 1) for odd in (0, 1) for g in range(4)]
    )
    blocks = jnp.arange(block_mask.shape[1], dtype=jnp.int32)
    key_hot = (key_ids[:, None] == blocks[None, :]).astype(jnp.float32)
    query_hot = (query_ids[:, None] == blocks[None, :]).astype(jnp.float32)
    mask = lax.dynamic_index_in_dim(block_mask, core, 0, keepdims=False).astype(jnp.float32)
    live = query_hot @ mask @ key_hot.T > 0.5
    live = live | (query_ids[:, None] == key_ids[None, :])
    bias = jnp.where(live, 0.0, NEG).astype(jnp.bfloat16)
    bias = jnp.pad(bias, ((0, 0), (0, HD - bias.shape[1])))
    bias = jnp.repeat(bias, BLOCK, axis=0)

    a_own = jnp.concatenate(direct(tokens[:half], "tensor", nt), axis=1)
    b_parts, w = hold((direct(tokens[half:], "ulysses", nu), w))
    b_own = jnp.concatenate(b_parts, axis=0)
    a_m = pp(a_own, "ulysses", ring(nu, 1))
    b_m = pp(b_own, "tensor", ring(nt, 1))
    a_p = pp(a_own, "ulysses", ring(nu, -1))
    b_p = pp(b_own, "tensor", ring(nt, -1))
    ah, bh = a_own.shape[0] // 2, b_own.shape[0] // 2
    a0 = pp(a_m[:ah], "ulysses", ring(nu, 1))
    a1 = pp(a_p[ah:], "ulysses", ring(nu, -1))
    b0 = pp(b_m[:bh], "tensor", ring(nt, 1))
    b1 = pp(b_p[bh:], "tensor", ring(nt, -1))

    def swap(kv, give):
        got = pp(give, "blk", core_swap(nb))
        return got[:, :HD], jnp.concatenate([kv, got[:, HD:]], axis=0)

    def near_y(kv):
        return [pp(kv, "blk", y_ring(nb, s)) for s in (1, -1)]

    def far_y(kv_m, kv_p):
        h = kv_m.shape[0] // 2
        return [pp(kv_m[:h], "blk", y_ring(nb, 1)), pp(kv_p[h:], "blk", y_ring(nb, -1))]

    done, part = project_stage(where, w, scale, [a_own], [b_own], (0,), None, None, False)
    done, bias, w_o = hold((done, bias, w_o))
    q1, kv1, give1, part = project_stage(
        where, w, scale, [a_m, a_p], [b_m, b_p], (1, 2), done, part, False
    )
    q1x, kv1 = swap(kv1, give1)
    kv1_near = near_y(kv1)
    q2, kv2, give2 = project_stage(where, w, scale, [a0, a1], [b0, b1], (3, 3), None, part, True)
    give2, kv1_near = hold((give2, kv1_near))
    q2x, kv2 = swap(kv2, give2)
    kv1_far = far_y(*kv1_near)
    kv2_near = near_y(kv2)
    kv2_far = far_y(*kv2_near)

    q = jnp.concatenate([q1, q2, q1x, q2x], axis=0)
    state = attention(q, bias, [kv1] + kv1_near, (768,) * 3, 0, None, False)
    state = attention(q, bias, kv1_far + [kv2], (384, 384, 640), 18, state, False)
    state = attention(q, bias, kv2_near, (640, 640), 34, state, False)
    out = attention(q, bias, kv2_far, (640, 640), 54, state, True)

    out = out.reshape(2, 2, nu, half, HD)
    other = pp(out[1], "blk", core_swap(nb))
    mine = out[0]
    first = jnp.where(core == 0, mine, other)
    second = jnp.where(core == 0, other, mine)
    heads = jnp.concatenate([first, second], axis=-1)
    heads = [heads[:, g].reshape(2 * half, 2 * HD) for g in range(nu)]
    arrived = [heads[0]] + [
        pp(heads[i], "ulysses", ring(nu, OFFSETS[i])) for i in range(1, nu)
    ]
    bf = jnp.bfloat16
    far_0, far_1 = out_project(where, arrived, w_o, (3,), bf, 2)
    rows = 2 * half
    hr = rows // 2
    far_m = pp(far_0, "tensor", ring(nt, 1))
    far_p = pp(far_1, "tensor", ring(nt, -1))
    to_m, to_p = out_project(where, arrived, w_o, (1, 2), jnp.float32, 1)
    to_p = jnp.concatenate([to_p[:hr] + far_m.astype(jnp.float32), to_p[hr:]], axis=0).astype(bf)
    to_m = jnp.concatenate([to_m[:hr], to_m[hr:] + far_p.astype(jnp.float32)], axis=0).astype(bf)
    from_m = pp(to_p, "tensor", ring(nt, 1))
    from_p = pp(to_m, "tensor", ring(nt, -1))
    (own,) = out_project(where, arrived, w_o, (0,), jnp.float32, 1)
    return (own + from_m.astype(jnp.float32) + from_p.astype(jnp.float32)).astype(bf)


def solution(mesh):
    return jax.shard_map(
        local,
        mesh=mesh,
        in_specs=(
            P(("ulysses", "blk"), "tensor"),
            P(None, None, ("ulysses", "tensor")),
            P(None, ("ulysses", "tensor")),
            P(("ulysses", "tensor"), None, None),
            P(None, "tensor", None),
        ),
        out_specs=P(("ulysses", "blk"), "tensor"),
        check_vma=False,
    )
```

```python
import functools
import math

import jax
import jax.numpy as jnp
from jax import lax
from jax.experimental import pallas as pl
from jax.experimental.pallas import tpu as pltpu
from jax.sharding import PartitionSpec as P

HD = 128
BLOCK = 128
NEG = -1e30
LOG2E = 1.4426950408889634
OFFSETS = (0, -1, 1, 2)
CONTRACT_LAST = (((1,), (1,)), ((), ()))


def ring(n, step):
    return [(i, (i + step) % n) for i in range(n)]


def y_ring(n, step):
    return [(i, (i + 2 * step) % n) for i in range(n)]


def core_swap(n):
    return [(i, i ^ 1) for i in range(n)]


def emit_heads(acc, scale_ref, core, q_ref, kv_ref, give_ref):
    scaled = (acc * scale_ref[...]).astype(jnp.bfloat16)
    heads = [[scaled[:, c * 256 + h * HD : c * 256 + (h + 1) * HD] for c in range(3)] for h in (0, 1)]
    is_first = core == 0

    @pl.when(is_first)
    def _():
        q_ref[...] = heads[0][0]
        kv_ref[...] = jnp.concatenate(heads[0][1:], axis=1)
        give_ref[...] = jnp.concatenate(heads[1], axis=1)

    @pl.when(jnp.logical_not(is_first))
    def _():
        q_ref[...] = heads[1][0]
        kv_ref[...] = jnp.concatenate(heads[1][1:], axis=1)
        give_ref[...] = jnp.concatenate(heads[0], axis=1)


def heads_shape(rows):
    return [jax.ShapeDtypeStruct((rows, n * HD), jnp.bfloat16) for n in (1, 2, 3)]


def stage_kernel(n_a, b_slices, n_done, has_part, emit_all, where_ref, w_ref, scale_ref, *refs):
    a_refs, refs = refs[:n_a], refs[n_a:]
    b_refs, refs = refs[: len(b_slices)], refs[len(b_slices) :]
    done_refs, refs = refs[:n_done], refs[n_done:]
    part_refs, refs = refs[:has_part], refs[has_part:]
    outs, acc_ref = refs[:-1], refs[-1]
    feat = w_ref.shape[1] // 4
    na = sum(r.shape[0] for r in a_refs)
    fresh = not has_part
    for i in range(4):
        at = pl.ds(pl.multiple_of(where_ref[i] * feat, feat), feat)
        x = [r[:, i * feat : (i + 1) * feat] for r in a_refs]
        x += [r[...] for r, s in zip(b_refs, b_slices) if s == i]
        with_b = len(x) > n_a
        x = jnp.concatenate(x, axis=0) if len(x) > 1 else x[0]
        for c in range(3):
            cols = slice(c * 256, (c + 1) * 256)
            d = jnp.dot(x, w_ref[c, at, :], preferred_element_type=jnp.float32)
            acc_ref[:na, cols] = d[:na] if i == 0 else acc_ref[:na, cols] + d[:na]
            if with_b:
                first = i == min(b_slices)
                before = None if first and fresh else part_refs[0][:, cols] if first else acc_ref[na:, cols]
                acc_ref[na:, cols] = d[na:] if before is None else before + d[na:]
    if not emit_all and not n_done:
        outs[0][...] = acc_ref[:na]
        outs[1][...] = acc_ref[na:]
        return
    rows = acc_ref[...] if emit_all else acc_ref[:na]
    if n_done:
        rows = jnp.concatenate([done_refs[0][...], rows], axis=0)
    emit_heads(rows, scale_ref, where_ref[4], *outs[:3])
    if not emit_all:
        outs[3][...] = acc_ref[na:]


VM = pl.BlockSpec(memory_space=pltpu.VMEM)
FIXED = [pl.BlockSpec(memory_space=pltpu.SMEM), VM, VM]


def project_stage(where, w, scale, a_parts, b_parts, b_slices, done, part, emit_all):
    feat = w.shape[1] // 4
    na = sum(x.shape[0] for x in a_parts)
    nb = 512 if part is None else part.shape[0]
    f32 = lambda n: jax.ShapeDtypeStruct((n, 768), jnp.float32)
    if emit_all:
        shapes = heads_shape(na + nb)
    elif done is not None:
        shapes = heads_shape(done.shape[0] + na) + [f32(nb)]
    else:
        shapes = [f32(na), f32(nb)]
    extra = [x for x in (done, part) if x is not None]
    return pl.pallas_call(
        functools.partial(
            stage_kernel, len(a_parts), b_slices, int(done is not None), int(part is not None), emit_all
        ),
        in_specs=FIXED + [VM] * (len(a_parts) + len(b_parts) + len(extra)),
        out_specs=[VM] * len(shapes),
        out_shape=shapes,
        scratch_shapes=[pltpu.VMEM((na + nb, 768), jnp.float32)],
        compiler_params=pltpu.CompilerParams(vmem_limit_bytes=16 << 20),
        cost_estimate=pl.CostEstimate(
            flops=2 * 768 * feat * (4 * na + sum(x.shape[0] for x in b_parts)),
            bytes_accessed=w.size * 2,
            transcendentals=0,
        ),
    )(where, w, scale, *a_parts, *b_parts, *extra)


def out_kernel(places, where_ref, *refs):
    xs, w_hbm, refs = refs[:4], refs[4], refs[5:]
    outs, (w_buf, sems) = refs[:-2], refs[-2:]
    cols = w_buf.shape[3]
    copies = []
    for n, place in enumerate(places):
        at = pl.ds(pl.multiple_of(where_ref[place] * cols, cols), cols)
        for i in range(4):
            copies.append(
                pltpu.make_async_copy(w_hbm.at[where_ref[5 + i], :, at], w_buf.at[n, i], sems.at[n, i])
            )
            copies[-1].start()
    per_place = len(outs) // len(places)
    for n in range(len(places)):
        d = None
        for i, x_ref in enumerate(xs):
            copies[4 * n + i].wait()
            more = jnp.dot(x_ref[...], w_buf[n, i], preferred_element_type=jnp.float32)
            d = more if d is None else d + more
        at = 0
        for o_ref in outs[n * per_place : (n + 1) * per_place]:
            o_ref[...] = d[at : at + o_ref.shape[0]].astype(o_ref.dtype)
            at += o_ref.shape[0]


def out_project(where, xs, w, places, dtype, pieces):
    rows, cols = xs[0].shape[0], w.shape[2] // 4
    n = len(places) * pieces
    return pl.pallas_call(
        functools.partial(out_kernel, places),
        in_specs=[pl.BlockSpec(memory_space=pltpu.SMEM)] + [VM] * 4 + [pl.BlockSpec(memory_space=pltpu.HBM)],
        out_specs=[VM] * n,
        out_shape=[jax.ShapeDtypeStruct((rows // pieces, cols), dtype)] * n,
        scratch_shapes=[
            pltpu.VMEM((len(places), 4, w.shape[1], cols), w.dtype),
            pltpu.SemaphoreType.DMA((len(places), 4)),
        ],
        compiler_params=pltpu.CompilerParams(vmem_limit_bytes=55 << 20),
        cost_estimate=pl.CostEstimate(
            flops=2 * len(places) * rows * 1024 * cols, bytes_accessed=n * 4 * rows * cols, transcendentals=0
        ),
    )(where, *xs, w)


def attn_kernel(sizes, first_block, begin, end, q_ref, qm_ref, *refs):
    if not begin:
        state_refs, refs = refs[:3], refs[3:]
    kv_refs, outs = refs[: len(sizes)], refs[len(sizes) :]
    rows = q_ref.shape[0]
    q = jnp.concatenate([q_ref[...], qm_ref[...]], axis=1)
    tiles = []
    for kv_ref, bk in zip(kv_refs, sizes):
        for j in range(0, kv_ref.shape[0], bk):
            tiles.append((kv_ref, slice(j, j + bk), bk, first_block))
            first_block += bk // BLOCK

    def score(tile):
        kv_ref, at, bk, block = tile
        lane = lax.broadcasted_iota(jnp.int32, (bk, HD), 1)
        inner = lax.broadcasted_iota(jnp.int32, (bk, HD), 0) // BLOCK
        onehot = (lane == inner + block).astype(jnp.float32).astype(jnp.bfloat16)
        k = jnp.concatenate([kv_ref[at, :HD], onehot], axis=1)
        return lax.dot_general(q, k, CONTRACT_LAST, preferred_element_type=jnp.float32)

    s = score(tiles[0])
    for i, (kv_ref, at, bk, _) in enumerate(tiles):
        s_next = score(tiles[i + 1]) if i + 1 < len(tiles) else None
        top = jnp.max(s, axis=1, keepdims=True)
        v = jnp.concatenate([kv_ref[at, HD:], jnp.ones((bk, HD), jnp.bfloat16)], axis=1)
        fresh = begin and i == 0
        if fresh:
            high = jnp.broadcast_to(top, (rows, HD))
        else:
            if i == 0:
                old = state_refs[2][...]
                acc = jnp.concatenate([state_refs[0][...], state_refs[1][...]], axis=1)
            else:
                old = high
            high = jnp.maximum(old, top)
        p = jnp.exp2(s - jnp.concatenate([high] * (bk // HD), axis=1)).astype(jnp.bfloat16)
        d = jnp.dot(p, v, preferred_element_type=jnp.float32)
        if fresh:
            acc = d
        else:
            factor = jnp.exp2(old - high)
            acc = acc * jnp.concatenate([factor, factor], axis=1) + d
        s = s_next
    if end:
        outs[0][...] = (acc[:, :HD] / acc[:, HD:]).astype(jnp.bfloat16)
    else:
        outs[0][...] = acc[:, :HD]
        outs[1][...] = acc[:, HD:]
        outs[2][...] = high


def attention(q, qm, kvs, sizes, first_block, state, end, bq=1024):
    rows = q.shape[0]
    keys = sum(kv.shape[0] for kv in kvs)
    begin = state is None
    block = pl.BlockSpec((bq, HD), lambda i: (i, 0))
    f32 = jax.ShapeDtypeStruct((rows, HD), jnp.float32)
    return pl.pallas_call(
        functools.partial(attn_kernel, sizes, first_block, begin, end),
        grid=(rows // bq,),
        in_specs=[block] * (2 if begin else 5)
        + [pl.BlockSpec(kv.shape, lambda i: (0, 0)) for kv in kvs],
        out_specs=block if end else [block] * 3,
        out_shape=jax.ShapeDtypeStruct((rows, HD), jnp.bfloat16) if end else [f32] * 3,
        compiler_params=pltpu.CompilerParams(vmem_limit_bytes=28 << 20),
        cost_estimate=pl.CostEstimate(
            flops=8 * rows * keys * HD, bytes_accessed=keys * 512, transcendentals=rows * keys
        ),
    )(q, qm, *([] if begin else state), *kvs)


def local(tokens, w_qkv, qkv_scale, block_mask, w_out):
    nu, nb, nt = lax.axis_size("ulysses"), lax.axis_size("blk"), lax.axis_size("tensor")
    u, b, t = lax.axis_index("ulysses"), lax.axis_index("blk"), lax.axis_index("tensor")
    y, core = b // 2, b % 2
    half = tokens.shape[0] // 2
    quarter = half // 2
    pp = lax.ppermute
    offsets = jnp.array(OFFSETS, jnp.int32)

    def direct(value, axis, n):
        return [value] + [pp(value, axis, ring(n, s)) for s in (1, -1, 2)]

    where = jnp.concatenate([(t + offsets) % nt, core[None], (u - offsets) % nu])
    w = jnp.transpose(w_qkv, (1, 0, 2))
    hold = lax.optimization_barrier
    scale = qkv_scale * jnp.array([LOG2E / math.sqrt(HD), 1.0, 1.0], jnp.float32)[:, None]
    scale = jnp.repeat(scale.reshape(1, 6), HD, axis=1)

    ny = nb // 2
    groups = (u + offsets) % nu
    cores = jnp.stack([core, 1 - core])

    def block_id(yy, slot, group, odd):
        return (groups[group] * nb + 2 * (yy % ny) + cores[slot]) * 2 + odd

    early = [(g, 0) for g in range(3)]
    late = [(3, 0)] + [(g, 1) for g in range(4)]
    def ring_order(part):
        own = [(y, s) + g for s in (0, 1) for g in part]
        near = [(y + o, s) + g for o in (-1, 1) for s in (0, 1) for g in part]
        far = [(y + 2, s) + g for s in (0, 1) for g in part]
        return own, near, far

    early_ids, late_ids = ring_order(early), ring_order(late)
    keys = early_ids[0] + early_ids[1] + late_ids[0] + late_ids[1] + early_ids[2] + late_ids[2]
    key_ids = jnp.stack([block_id(*k) for k in keys])
    query_ids = jnp.stack(
        [block_id(y, s, g, odd) for s in (0, 1) for odd in (0, 1) for g in range(4)]
    )
    blocks = jnp.arange(block_mask.shape[1], dtype=jnp.int32)
    key_hot = (key_ids[:, None] == blocks[None, :]).astype(jnp.float32)
    query_hot = (query_ids[:, None] == blocks[None, :]).astype(jnp.float32)
    mask = lax.dynamic_index_in_dim(block_mask, core, 0, keepdims=False).astype(jnp.float32)
    live = query_hot @ mask @ key_hot.T > 0.5
    live = live | (query_ids[:, None] == key_ids[None, :])
    bias = jnp.where(live, 0.0, NEG).astype(jnp.bfloat16)
    bias = jnp.pad(bias, ((0, 0), (0, HD - bias.shape[1])))
    bias = jnp.repeat(bias, BLOCK, axis=0)

    a_parts = direct(tokens[:half], "tensor", nt)
    b_parts = direct(tokens[half:], "ulysses", nu)
    a_own = jnp.concatenate(a_parts, axis=1)
    b_own = jnp.concatenate(b_parts, axis=0)
    a_m = pp(a_own, "ulysses", ring(nu, 1))
    b_m = pp(b_own, "tensor", ring(nt, 1))
    a_p = pp(a_own, "ulysses", ring(nu, -1))
    b_p = pp(b_own, "tensor", ring(nt, -1))
    done, part = project_stage(where, w, scale, [a_own], [b_own], (0,), None, None, False)
    done, bias = hold((done, bias))
    a_m, a_p, b_m, b_p = [hold((x, done))[0] for x in (a_m, a_p, b_m, b_p)]
    ah, bh = a_own.shape[0] // 2, b_own.shape[0] // 2
    a0 = pp(a_m[:ah], "ulysses", ring(nu, 1))
    a1 = pp(a_p[ah:], "ulysses", ring(nu, -1))
    b0 = pp(b_m[:bh], "tensor", ring(nt, 1))
    b1 = pp(b_p[bh:], "tensor", ring(nt, -1))

    def swap(kv, give):
        got = pp(give, "blk", core_swap(nb))
        return got[:, :HD], jnp.concatenate([kv, got[:, HD:]], axis=0)

    def near_y(kv):
        return [pp(kv, "blk", y_ring(nb, s)) for s in (1, -1)]

    def far_y(kv_m, kv_p):
        h = kv_m.shape[0] // 2
        return [pp(kv_m[:h], "blk", y_ring(nb, 1)), pp(kv_p[h:], "blk", y_ring(nb, -1))]

    q1, kv1, give1, part = project_stage(
        where, w, scale, [a_m, a_p], [b_m, b_p], (1, 2), done, part, False
    )
    q1x, kv1 = swap(kv1, give1)
    kv1_near = near_y(kv1)
    q2, kv2, give2 = project_stage(where, w, scale, [a0, a1], [b0, b1], (3, 3), None, part, True)
    give2, kv1_near = hold((give2, kv1_near))
    q2x, kv2 = swap(kv2, give2)
    kv2_near = near_y(kv2)
    q = jnp.concatenate([q1, q2, q1x, q2x], axis=0)
    q, kv1_near = hold((q, kv1_near))
    kv1_far = far_y(*kv1_near)
    kv2_far = far_y(*kv2_near)

    state = attention(q, bias, [kv1] + kv1_near + [kv2], (768, 768, 768, 640), 0, None, False)
    state = attention(q, bias, kv2_near + kv1_far, (640, 640, 384, 384), 28, state, False)
    out = attention(q, bias, kv2_far, (640, 640), 54, state, True)

    out = out.reshape(2, 2, nu, half, HD)
    other = pp(out[1], "blk", core_swap(nb))
    mine = out[0]
    first = jnp.where(core == 0, mine, other)
    second = jnp.where(core == 0, other, mine)
    heads = jnp.concatenate([first, second], axis=-1)
    heads = [heads[:, g].reshape(2 * half, 2 * HD) for g in range(nu)]
    arrived = [heads[0]] + [
        pp(heads[i], "ulysses", ring(nu, OFFSETS[i])) for i in range(1, nu)
    ]
    bf = jnp.bfloat16
    far_0, far_1 = out_project(where, arrived, w_out, (3,), bf, 2)
    rows = 2 * half
    hr = rows // 2
    far_m = pp(far_0, "tensor", ring(nt, 1))
    far_p = pp(far_1, "tensor", ring(nt, -1))
    to_m, to_p = out_project(where, arrived, w_out, (1, 2), jnp.float32, 1)
    to_p = jnp.concatenate([to_p[:hr] + far_m.astype(jnp.float32), to_p[hr:]], axis=0).astype(bf)
    to_m = jnp.concatenate([to_m[:hr], to_m[hr:] + far_p.astype(jnp.float32)], axis=0).astype(bf)
    from_m = pp(to_p, "tensor", ring(nt, 1))
    from_p = pp(to_m, "tensor", ring(nt, -1))
    (own,) = out_project(where, arrived, w_out, (0,), jnp.float32, 1)
    return (own + from_m.astype(jnp.float32) + from_p.astype(jnp.float32)).astype(bf)


def solution(mesh):
    return jax.shard_map(
        local,
        mesh=mesh,
        in_specs=(
            P(("ulysses", "blk"), "tensor"),
            P(None, None, ("ulysses", "tensor")),
            P(None, ("ulysses", "tensor")),
            P(("ulysses", "tensor"), None, None),
            P(None, "tensor", None),
        ),
        out_specs=P(("ulysses", "blk"), "tensor"),
        check_vma=False,
    )
```

```python
import functools
import math

import jax
import jax.numpy as jnp
from jax import lax
from jax.experimental import pallas as pl
from jax.experimental.pallas import tpu as pltpu
from jax.sharding import PartitionSpec as P

HD = 128
BLOCK = 128
NEG = -1e30
LOG2E = 1.4426950408889634
OFFSETS = (0, -1, 1, 2)
CONTRACT_LAST = (((1,), (1,)), ((), ()))


def ring(n, step):
    return [(i, (i + step) % n) for i in range(n)]


def y_ring(n, step):
    return [(i, (i + 2 * step) % n) for i in range(n)]


def core_swap(n):
    return [(i, i ^ 1) for i in range(n)]


def emit_heads(acc, scale_ref, core, q_ref, kv_ref, give_ref):
    scaled = (acc * scale_ref[...]).astype(jnp.bfloat16)
    heads = [[scaled[:, c * 256 + h * HD : c * 256 + (h + 1) * HD] for c in range(3)] for h in (0, 1)]
    is_first = core == 0

    @pl.when(is_first)
    def _():
        q_ref[...] = heads[0][0]
        kv_ref[...] = jnp.concatenate(heads[0][1:], axis=1)
        give_ref[...] = jnp.concatenate(heads[1], axis=1)

    @pl.when(jnp.logical_not(is_first))
    def _():
        q_ref[...] = heads[1][0]
        kv_ref[...] = jnp.concatenate(heads[1][1:], axis=1)
        give_ref[...] = jnp.concatenate(heads[0], axis=1)


def heads_shape(rows):
    return [jax.ShapeDtypeStruct((rows, n * HD), jnp.bfloat16) for n in (1, 2, 3)]


def load_kernel(where_ref, x_ref, hbm, o_ref, sems):
    width = o_ref.shape[3]
    copies = []
    for i in range(4):
        cols = pl.ds(pl.multiple_of(where_ref[i] * width, width), width)
        copies.append(pltpu.make_async_copy(hbm.at[:, :, cols], o_ref.at[i], sems.at[i]))
        copies[-1].start()
    for copy in copies:
        copy.wait()


def load_columns(where, w, x):
    return pl.pallas_call(
        load_kernel,
        in_specs=[pl.BlockSpec(memory_space=pltpu.SMEM), VM, pl.BlockSpec(memory_space=pltpu.HBM)],
        out_specs=VM,
        out_shape=jax.ShapeDtypeStruct((4,) + w.shape[:2] + (w.shape[2] // 4,), w.dtype),
        scratch_shapes=[pltpu.SemaphoreType.DMA((4,))],
        compiler_params=pltpu.CompilerParams(vmem_limit_bytes=40 << 20),
        cost_estimate=pl.CostEstimate(flops=0, bytes_accessed=w.size * 4, transcendentals=0),
    )(where, x, w)


def stage_kernel(n_a, b_slices, n_done, has_part, emit_all, where_ref, w_ref, scale_ref, *refs):
    a_refs, refs = refs[:n_a], refs[n_a:]
    b_refs, refs = refs[: len(b_slices)], refs[len(b_slices) :]
    done_refs, refs = refs[:n_done], refs[n_done:]
    part_refs, refs = refs[:has_part], refs[has_part:]
    outs, acc_ref = refs[:-1], refs[-1]
    feat = w_ref.shape[1] // 4
    na = sum(r.shape[0] for r in a_refs)
    fresh = not has_part
    for i in range(4):
        at = pl.ds(pl.multiple_of(where_ref[i] * feat, feat), feat)
        x = [r[:, i * feat : (i + 1) * feat] for r in a_refs]
        x += [r[...] for r, s in zip(b_refs, b_slices) if s == i]
        with_b = len(x) > n_a
        x = jnp.concatenate(x, axis=0) if len(x) > 1 else x[0]
        for c in range(3):
            cols = slice(c * 256, (c + 1) * 256)
            d = jnp.dot(x, w_ref[c, at, :], preferred_element_type=jnp.float32)
            acc_ref[:na, cols] = d[:na] if i == 0 else acc_ref[:na, cols] + d[:na]
            if with_b:
                first = i == min(b_slices)
                before = None if first and fresh else part_refs[0][:, cols] if first else acc_ref[na:, cols]
                acc_ref[na:, cols] = d[na:] if before is None else before + d[na:]
    if not emit_all and not n_done:
        outs[0][...] = acc_ref[:na]
        outs[1][...] = acc_ref[na:]
        return
    rows = acc_ref[...] if emit_all else acc_ref[:na]
    if n_done:
        rows = jnp.concatenate([done_refs[0][...], rows], axis=0)
    emit_heads(rows, scale_ref, where_ref[4], *outs[:3])
    if not emit_all:
        outs[3][...] = acc_ref[na:]


VM = pl.BlockSpec(memory_space=pltpu.VMEM)
FIXED = [pl.BlockSpec(memory_space=pltpu.SMEM), VM, VM]


def project_stage(where, w, scale, a_parts, b_parts, b_slices, done, part, emit_all):
    feat = w.shape[1] // 4
    na = sum(x.shape[0] for x in a_parts)
    nb = 512 if part is None else part.shape[0]
    f32 = lambda n: jax.ShapeDtypeStruct((n, 768), jnp.float32)
    if emit_all:
        shapes = heads_shape(na + nb)
    elif done is not None:
        shapes = heads_shape(done.shape[0] + na) + [f32(nb)]
    else:
        shapes = [f32(na), f32(nb)]
    extra = [x for x in (done, part) if x is not None]
    return pl.pallas_call(
        functools.partial(
            stage_kernel, len(a_parts), b_slices, int(done is not None), int(part is not None), emit_all
        ),
        in_specs=FIXED + [VM] * (len(a_parts) + len(b_parts) + len(extra)),
        out_specs=[VM] * len(shapes),
        out_shape=shapes,
        scratch_shapes=[pltpu.VMEM((na + nb, 768), jnp.float32)],
        compiler_params=pltpu.CompilerParams(vmem_limit_bytes=16 << 20),
        cost_estimate=pl.CostEstimate(
            flops=2 * 768 * feat * (4 * na + sum(x.shape[0] for x in b_parts)),
            bytes_accessed=w.size * 2,
            transcendentals=0,
        ),
    )(where, w, scale, *a_parts, *b_parts, *extra)


def out_kernel(places, where_ref, *refs):
    xs, w_ref, outs = refs[:4], refs[4], refs[5:]
    per_place = len(outs) // len(places)
    for n, place in enumerate(places):
        d = sum(
            jnp.dot(x_ref[...], w_ref[place, where_ref[5 + i]], preferred_element_type=jnp.float32)
            for i, x_ref in enumerate(xs)
        )
        at = 0
        for o_ref in outs[n * per_place : (n + 1) * per_place]:
            o_ref[...] = d[at : at + o_ref.shape[0]].astype(o_ref.dtype)
            at += o_ref.shape[0]


def out_project(where, xs, w, places, dtype, pieces):
    rows, cols = xs[0].shape[0], w.shape[3]
    n = len(places) * pieces
    return pl.pallas_call(
        functools.partial(out_kernel, places),
        in_specs=[pl.BlockSpec(memory_space=pltpu.SMEM)] + [VM] * 5,
        out_specs=[VM] * n,
        out_shape=[jax.ShapeDtypeStruct((rows // pieces, cols), dtype)] * n,
        compiler_params=pltpu.CompilerParams(vmem_limit_bytes=16 << 20),
        cost_estimate=pl.CostEstimate(
            flops=2 * len(places) * rows * 1024 * cols, bytes_accessed=n * 4 * rows * cols, transcendentals=0
        ),
    )(where, *xs, w)


def attn_kernel(sizes, first_block, begin, end, q_ref, qm_ref, *refs):
    if not begin:
        state_refs, refs = refs[:3], refs[3:]
    kv_refs, outs = refs[: len(sizes)], refs[len(sizes) :]
    rows = q_ref.shape[0]
    q = jnp.concatenate([q_ref[...], qm_ref[...]], axis=1)
    tiles = []
    for kv_ref, bk in zip(kv_refs, sizes):
        for j in range(0, kv_ref.shape[0], bk):
            tiles.append((kv_ref, slice(j, j + bk), bk, first_block))
            first_block += bk // BLOCK

    def score(tile):
        kv_ref, at, bk, block = tile
        lane = lax.broadcasted_iota(jnp.int32, (bk, HD), 1)
        inner = lax.broadcasted_iota(jnp.int32, (bk, HD), 0) // BLOCK
        onehot = (lane == inner + block).astype(jnp.float32).astype(jnp.bfloat16)
        k = jnp.concatenate([kv_ref[at, :HD], onehot], axis=1)
        return lax.dot_general(q, k, CONTRACT_LAST, preferred_element_type=jnp.float32)

    s = score(tiles[0])
    for i, (kv_ref, at, bk, _) in enumerate(tiles):
        s_next = score(tiles[i + 1]) if i + 1 < len(tiles) else None
        top = jnp.max(s, axis=1, keepdims=True)
        v = jnp.concatenate([kv_ref[at, HD:], jnp.ones((bk, HD), jnp.bfloat16)], axis=1)
        fresh = begin and i == 0
        if fresh:
            high = jnp.broadcast_to(top, (rows, HD))
        else:
            if i == 0:
                old = state_refs[2][...]
                acc = jnp.concatenate([state_refs[0][...], state_refs[1][...]], axis=1)
            else:
                old = high
            high = jnp.maximum(old, top)
        p = jnp.exp2(s - jnp.concatenate([high] * (bk // HD), axis=1)).astype(jnp.bfloat16)
        d = jnp.dot(p, v, preferred_element_type=jnp.float32)
        if fresh:
            acc = d
        else:
            factor = jnp.exp2(old - high)
            acc = acc * jnp.concatenate([factor, factor], axis=1) + d
        s = s_next
    if end:
        outs[0][...] = (acc[:, :HD] / acc[:, HD:]).astype(jnp.bfloat16)
    else:
        outs[0][...] = acc[:, :HD]
        outs[1][...] = acc[:, HD:]
        outs[2][...] = high


def attention(q, qm, kvs, sizes, first_block, state, end, bq=1024):
    rows = q.shape[0]
    keys = sum(kv.shape[0] for kv in kvs)
    begin = state is None
    block = pl.BlockSpec((bq, HD), lambda i: (i, 0))
    f32 = jax.ShapeDtypeStruct((rows, HD), jnp.float32)
    return pl.pallas_call(
        functools.partial(attn_kernel, sizes, first_block, begin, end),
        grid=(rows // bq,),
        in_specs=[block] * (2 if begin else 5)
        + [pl.BlockSpec(kv.shape, lambda i: (0, 0)) for kv in kvs],
        out_specs=block if end else [block] * 3,
        out_shape=jax.ShapeDtypeStruct((rows, HD), jnp.bfloat16) if end else [f32] * 3,
        compiler_params=pltpu.CompilerParams(vmem_limit_bytes=28 << 20),
        cost_estimate=pl.CostEstimate(
            flops=8 * rows * keys * HD, bytes_accessed=keys * 512, transcendentals=rows * keys
        ),
    )(q, qm, *([] if begin else state), *kvs)


def local(tokens, w_qkv, qkv_scale, block_mask, w_out):
    nu, nb, nt = lax.axis_size("ulysses"), lax.axis_size("blk"), lax.axis_size("tensor")
    u, b, t = lax.axis_index("ulysses"), lax.axis_index("blk"), lax.axis_index("tensor")
    y, core = b // 2, b % 2
    half = tokens.shape[0] // 2
    quarter = half // 2
    pp = lax.ppermute
    offsets = jnp.array(OFFSETS, jnp.int32)

    def direct(value, axis, n):
        return [value] + [pp(value, axis, ring(n, s)) for s in (1, -1, 2)]

    where = jnp.concatenate([(t + offsets) % nt, core[None], (u - offsets) % nu])
    w = jnp.transpose(w_qkv, (1, 0, 2))
    hold = lax.optimization_barrier
    scale = qkv_scale * jnp.array([LOG2E / math.sqrt(HD), 1.0, 1.0], jnp.float32)[:, None]
    scale = jnp.repeat(scale.reshape(1, 6), HD, axis=1)

    ny = nb // 2
    groups = (u + offsets) % nu
    cores = jnp.stack([core, 1 - core])

    def block_id(yy, slot, group, odd):
        return (groups[group] * nb + 2 * (yy % ny) + cores[slot]) * 2 + odd

    early = [(g, 0) for g in range(3)]
    late = [(3, 0)] + [(g, 1) for g in range(4)]
    def ring_order(part):
        own = [(y, s) + g for s in (0, 1) for g in part]
        near = [(y + o, s) + g for o in (-1, 1) for s in (0, 1) for g in part]
        far = [(y + 2, s) + g for s in (0, 1) for g in part]
        return own, near, far

    early_ids, late_ids = ring_order(early), ring_order(late)
    keys = sum(early_ids, []) + sum(late_ids, [])
    key_ids = jnp.stack([block_id(*k) for k in keys])
    query_ids = jnp.stack(
        [block_id(y, s, g, odd) for s in (0, 1) for odd in (0, 1) for g in range(4)]
    )
    blocks = jnp.arange(block_mask.shape[1], dtype=jnp.int32)
    key_hot = (key_ids[:, None] == blocks[None, :]).astype(jnp.float32)
    query_hot = (query_ids[:, None] == blocks[None, :]).astype(jnp.float32)
    mask = lax.dynamic_index_in_dim(block_mask, core, 0, keepdims=False).astype(jnp.float32)
    live = query_hot @ mask @ key_hot.T > 0.5
    live = live | (query_ids[:, None] == key_ids[None, :])
    bias = jnp.where(live, 0.0, NEG).astype(jnp.bfloat16)
    bias = jnp.pad(bias, ((0, 0), (0, HD - bias.shape[1])))
    bias = jnp.repeat(bias, BLOCK, axis=0)

    a_own = jnp.concatenate(direct(tokens[:half], "tensor", nt), axis=1)
    b_own = jnp.concatenate(direct(tokens[half:], "ulysses", nu), axis=0)
    a_m = pp(a_own, "ulysses", ring(nu, 1))
    b_m = pp(b_own, "tensor", ring(nt, 1))
    a_p = pp(a_own, "ulysses", ring(nu, -1))
    b_p = pp(b_own, "tensor", ring(nt, -1))
    ah, bh = a_own.shape[0] // 2, b_own.shape[0] // 2
    a0 = pp(a_m[:ah], "ulysses", ring(nu, 1))
    a1 = pp(a_p[ah:], "ulysses", ring(nu, -1))
    b0 = pp(b_m[:bh], "tensor", ring(nt, 1))
    b1 = pp(b_p[bh:], "tensor", ring(nt, -1))

    def swap(kv, give):
        got = pp(give, "blk", core_swap(nb))
        return got[:, :HD], jnp.concatenate([kv, got[:, HD:]], axis=0)

    def near_y(kv):
        return [pp(kv, "blk", y_ring(nb, s)) for s in (1, -1)]

    def far_y(kv_m, kv_p):
        h = kv_m.shape[0] // 2
        return [pp(kv_m[:h], "blk", y_ring(nb, 1)), pp(kv_p[h:], "blk", y_ring(nb, -1))]

    done, part = project_stage(where, w, scale, [a_own], [b_own], (0,), None, None, False)
    done, bias = hold((done, bias))
    q1, kv1, give1, part = project_stage(
        where, w, scale, [a_m, a_p], [b_m, b_p], (1, 2), done, part, False
    )
    q1x, kv1 = swap(kv1, give1)
    kv1_near = near_y(kv1)
    q2, kv2, give2 = project_stage(where, w, scale, [a0, a1], [b0, b1], (3, 3), None, part, True)
    give2, kv1_near = hold((give2, kv1_near))
    q2x, kv2 = swap(kv2, give2)
    kv1_far = far_y(*kv1_near)
    kv2_near = near_y(kv2)
    kv2_far = far_y(*kv2_near)

    q = jnp.concatenate([q1, q2, q1x, q2x], axis=0)
    state = attention(q, bias, [kv1] + kv1_near, (768,) * 3, 0, None, False)
    state = attention(q, bias, kv1_far + [kv2], (384, 384, 640), 18, state, False)
    state = attention(q, bias, kv2_near, (640, 640), 34, state, False)
    out = attention(q, bias, kv2_far, (640, 640), 54, state, True)

    out = out.reshape(2, 2, nu, half, HD)
    other = pp(out[1], "blk", core_swap(nb))
    mine = out[0]
    first = jnp.where(core == 0, mine, other)
    second = jnp.where(core == 0, other, mine)
    heads = jnp.concatenate([first, second], axis=-1)
    heads = [heads[:, g].reshape(2 * half, 2 * HD) for g in range(nu)]
    arrived = [heads[0]] + [
        pp(heads[i], "ulysses", ring(nu, OFFSETS[i])) for i in range(1, nu)
    ]
    w_o = load_columns(where, w_out, heads[0])
    bf = jnp.bfloat16
    far_0, far_1 = out_project(where, arrived, w_o, (3,), bf, 2)
    rows = 2 * half
    hr = rows // 2
    far_m = pp(far_0, "tensor", ring(nt, 1))
    far_p = pp(far_1, "tensor", ring(nt, -1))
    to_m, to_p = out_project(where, arrived, w_o, (1, 2), jnp.float32, 1)
    to_p = jnp.concatenate([to_p[:hr] + far_m.astype(jnp.float32), to_p[hr:]], axis=0).astype(bf)
    to_m = jnp.concatenate([to_m[:hr], to_m[hr:] + far_p.astype(jnp.float32)], axis=0).astype(bf)
    from_m = pp(to_p, "tensor", ring(nt, 1))
    from_p = pp(to_m, "tensor", ring(nt, -1))
    (own,) = out_project(where, arrived, w_o, (0,), jnp.float32, 1)
    return (own + from_m.astype(jnp.float32) + from_p.astype(jnp.float32)).astype(bf)


def solution(mesh):
    return jax.shard_map(
        local,
        mesh=mesh,
        in_specs=(
            P(("ulysses", "blk"), "tensor"),
            P(None, None, ("ulysses", "tensor")),
            P(None, ("ulysses", "tensor")),
            P(("ulysses", "tensor"), None, None),
            P(None, "tensor", None),
        ),
        out_specs=P(("ulysses", "blk"), "tensor"),
        check_vma=False,
    )
```

```python
import functools
import math

import jax
import jax.numpy as jnp
from jax import lax
from jax.experimental import pallas as pl
from jax.experimental.pallas import tpu as pltpu
from jax.sharding import PartitionSpec as P

HD = 128
BLOCK = 128
NEG = -1e30
LOG2E = 1.4426950408889634
OFFSETS = (0, -1, 1, 2)
CONTRACT_LAST = (((1,), (1,)), ((), ()))


def ring(n, step):
    return [(i, (i + step) % n) for i in range(n)]


def y_ring(n, step):
    return [(i, (i + 2 * step) % n) for i in range(n)]


def core_swap(n):
    return [(i, i ^ 1) for i in range(n)]


def emit_heads(acc, scale_ref, core, q_ref, kv_ref, give_ref):
    scaled = (acc * scale_ref[...]).astype(jnp.bfloat16)
    heads = [[scaled[:, c * 256 + h * HD : c * 256 + (h + 1) * HD] for c in range(3)] for h in (0, 1)]
    is_first = core == 0

    @pl.when(is_first)
    def _():
        q_ref[...] = heads[0][0]
        kv_ref[...] = jnp.concatenate(heads[0][1:], axis=1)
        give_ref[...] = jnp.concatenate(heads[1], axis=1)

    @pl.when(jnp.logical_not(is_first))
    def _():
        q_ref[...] = heads[1][0]
        kv_ref[...] = jnp.concatenate(heads[1][1:], axis=1)
        give_ref[...] = jnp.concatenate(heads[0], axis=1)


def heads_shape(rows):
    return [jax.ShapeDtypeStruct((rows, n * HD), jnp.bfloat16) for n in (1, 2, 3)]


def load_kernel(where_ref, x_ref, hbm, o_ref, sems):
    width = o_ref.shape[3]
    copies = []
    for i in range(4):
        cols = pl.ds(pl.multiple_of(where_ref[i] * width, width), width)
        copies.append(pltpu.make_async_copy(hbm.at[:, :, cols], o_ref.at[i], sems.at[i]))
        copies[-1].start()
    for copy in copies:
        copy.wait()


def load_columns(where, w, x):
    return pl.pallas_call(
        load_kernel,
        in_specs=[pl.BlockSpec(memory_space=pltpu.SMEM), VM, pl.BlockSpec(memory_space=pltpu.HBM)],
        out_specs=VM,
        out_shape=jax.ShapeDtypeStruct((4,) + w.shape[:2] + (w.shape[2] // 4,), w.dtype),
        scratch_shapes=[pltpu.SemaphoreType.DMA((4,))],
        compiler_params=pltpu.CompilerParams(vmem_limit_bytes=40 << 20),
        cost_estimate=pl.CostEstimate(flops=0, bytes_accessed=w.size * 4, transcendentals=0),
    )(where, x, w)


def stage_kernel(n_a, b_slices, n_done, has_part, emit_all, where_ref, w_ref, scale_ref, *refs):
    a_refs, refs = refs[:n_a], refs[n_a:]
    b_refs, refs = refs[: len(b_slices)], refs[len(b_slices) :]
    done_refs, refs = refs[:n_done], refs[n_done:]
    part_refs, refs = refs[:has_part], refs[has_part:]
    outs, acc_ref = refs[:-1], refs[-1]
    feat = w_ref.shape[1] // 4
    na = sum(r.shape[0] for r in a_refs)
    fresh = not has_part
    for i in range(4):
        at = pl.ds(pl.multiple_of(where_ref[i] * feat, feat), feat)
        x = [r[:, i * feat : (i + 1) * feat] for r in a_refs]
        x += [r[...] for r, s in zip(b_refs, b_slices) if s == i]
        with_b = len(x) > n_a
        x = jnp.concatenate(x, axis=0) if len(x) > 1 else x[0]
        for c in range(3):
            cols = slice(c * 256, (c + 1) * 256)
            d = jnp.dot(x, w_ref[c, at, :], preferred_element_type=jnp.float32)
            acc_ref[:na, cols] = d[:na] if i == 0 else acc_ref[:na, cols] + d[:na]
            if with_b:
                first = i == min(b_slices)
                before = None if first and fresh else part_refs[0][:, cols] if first else acc_ref[na:, cols]
                acc_ref[na:, cols] = d[na:] if before is None else before + d[na:]
    if not emit_all and not n_done:
        outs[0][...] = acc_ref[:na]
        outs[1][...] = acc_ref[na:]
        return
    rows = acc_ref[...] if emit_all else acc_ref[:na]
    if n_done:
        rows = jnp.concatenate([done_refs[0][...], rows], axis=0)
    emit_heads(rows, scale_ref, where_ref[4], *outs[:3])
    if not emit_all and b_slices:
        outs[3][...] = acc_ref[na:]


def part_kernel(b_slices, where_ref, w_ref, part_ref, *refs):
    b_refs, o_ref = refs[:-1], refs[-1]
    feat = w_ref.shape[1] // 4
    for c in range(3):
        cols = slice(c * 256, (c + 1) * 256)
        d = part_ref[:, cols]
        for i, b_ref in zip(b_slices, b_refs):
            at = pl.ds(pl.multiple_of(where_ref[i] * feat, feat), feat)
            d = d + jnp.dot(b_ref[...], w_ref[c, at, :], preferred_element_type=jnp.float32)
        o_ref[:, cols] = d


def project_part(where, w, b_parts, b_slices, part):
    return pl.pallas_call(
        functools.partial(part_kernel, b_slices),
        in_specs=FIXED[:2] + [VM] * (1 + len(b_parts)),
        out_specs=VM,
        out_shape=jax.ShapeDtypeStruct(part.shape, part.dtype),
        compiler_params=pltpu.CompilerParams(vmem_limit_bytes=16 << 20),
        cost_estimate=pl.CostEstimate(
            flops=2 * 768 * sum(x.size for x in b_parts), bytes_accessed=w.size, transcendentals=0
        ),
    )(where, w, part, *b_parts)


VM = pl.BlockSpec(memory_space=pltpu.VMEM)
FIXED = [pl.BlockSpec(memory_space=pltpu.SMEM), VM, VM]


def project_stage(where, w, scale, a_parts, b_parts, b_slices, done, part, emit_all):
    feat = w.shape[1] // 4
    na = sum(x.shape[0] for x in a_parts)
    nb = part.shape[0] if part is not None else b_parts[0].shape[0] if b_parts else 0
    f32 = lambda n: jax.ShapeDtypeStruct((n, 768), jnp.float32)
    if emit_all:
        shapes = heads_shape(na + nb)
    elif done is not None:
        shapes = heads_shape(done.shape[0] + na) + ([f32(nb)] if b_parts else [])
    else:
        shapes = [f32(na), f32(nb)]
    extra = [x for x in (done, part) if x is not None]
    return pl.pallas_call(
        functools.partial(
            stage_kernel, len(a_parts), b_slices, int(done is not None), int(part is not None), emit_all
        ),
        in_specs=FIXED + [VM] * (len(a_parts) + len(b_parts) + len(extra)),
        out_specs=[VM] * len(shapes),
        out_shape=shapes,
        scratch_shapes=[pltpu.VMEM((na + nb, 768), jnp.float32)],
        compiler_params=pltpu.CompilerParams(vmem_limit_bytes=16 << 20),
        cost_estimate=pl.CostEstimate(
            flops=2 * 768 * feat * (4 * na + sum(x.shape[0] for x in b_parts)),
            bytes_accessed=w.size * 2,
            transcendentals=0,
        ),
    )(where, w, scale, *a_parts, *b_parts, *extra)


def out_kernel(places, where_ref, *refs):
    xs, w_ref, outs = refs[:4], refs[4], refs[5:]
    per_place = len(outs) // len(places)
    for n, place in enumerate(places):
        d = sum(
            jnp.dot(x_ref[...], w_ref[place, where_ref[5 + i]], preferred_element_type=jnp.float32)
            for i, x_ref in enumerate(xs)
        )
        at = 0
        for o_ref in outs[n * per_place : (n + 1) * per_place]:
            o_ref[...] = d[at : at + o_ref.shape[0]].astype(o_ref.dtype)
            at += o_ref.shape[0]


def out_project(where, xs, w, places, dtype, pieces):
    rows, cols = xs[0].shape[0], w.shape[3]
    n = len(places) * pieces
    return pl.pallas_call(
        functools.partial(out_kernel, places),
        in_specs=[pl.BlockSpec(memory_space=pltpu.SMEM)] + [VM] * 5,
        out_specs=[VM] * n,
        out_shape=[jax.ShapeDtypeStruct((rows // pieces, cols), dtype)] * n,
        compiler_params=pltpu.CompilerParams(vmem_limit_bytes=16 << 20),
        cost_estimate=pl.CostEstimate(
            flops=2 * len(places) * rows * 1024 * cols, bytes_accessed=n * 4 * rows * cols, transcendentals=0
        ),
    )(where, *xs, w)


def attn_kernel(sizes, first_block, begin, end, q_ref, qm_ref, *refs):
    if not begin:
        state_refs, refs = refs[:3], refs[3:]
    kv_refs, outs = refs[: len(sizes)], refs[len(sizes) :]
    rows = q_ref.shape[0]
    q = jnp.concatenate([q_ref[...], qm_ref[...]], axis=1)
    tiles = []
    for kv_ref, bk in zip(kv_refs, sizes):
        for j in range(0, kv_ref.shape[0], bk):
            tiles.append((kv_ref, slice(j, j + bk), bk, first_block))
            first_block += bk // BLOCK

    def score(tile):
        kv_ref, at, bk, block = tile
        lane = lax.broadcasted_iota(jnp.int32, (bk, HD), 1)
        inner = lax.broadcasted_iota(jnp.int32, (bk, HD), 0) // BLOCK
        onehot = (lane == inner + block).astype(jnp.float32).astype(jnp.bfloat16)
        k = jnp.concatenate([kv_ref[at, :HD], onehot], axis=1)
        return lax.dot_general(q, k, CONTRACT_LAST, preferred_element_type=jnp.float32)

    s = score(tiles[0])
    for i, (kv_ref, at, bk, _) in enumerate(tiles):
        s_next = score(tiles[i + 1]) if i + 1 < len(tiles) else None
        top = jnp.max(s, axis=1, keepdims=True)
        v = jnp.concatenate([kv_ref[at, HD:], jnp.ones((bk, HD), jnp.bfloat16)], axis=1)
        fresh = begin and i == 0
        if fresh:
            high = jnp.broadcast_to(top, (rows, HD))
        else:
            if i == 0:
                old = state_refs[2][...]
                acc = jnp.concatenate([state_refs[0][...], state_refs[1][...]], axis=1)
            else:
                old = high
            high = jnp.maximum(old, top)
        p = jnp.exp2(s - jnp.concatenate([high] * (bk // HD), axis=1)).astype(jnp.bfloat16)
        d = jnp.dot(p, v, preferred_element_type=jnp.float32)
        if fresh:
            acc = d
        else:
            factor = jnp.exp2(old - high)
            acc = acc * jnp.concatenate([factor, factor], axis=1) + d
        s = s_next
    if end:
        outs[0][...] = (acc[:, :HD] / acc[:, HD:]).astype(jnp.bfloat16)
    else:
        outs[0][...] = acc[:, :HD]
        outs[1][...] = acc[:, HD:]
        outs[2][...] = high


def attention(q, qm, kvs, sizes, first_block, state, end, bq=1024):
    rows = q.shape[0]
    keys = sum(kv.shape[0] for kv in kvs)
    begin = state is None
    block = pl.BlockSpec((bq, HD), lambda i: (i, 0))
    f32 = jax.ShapeDtypeStruct((rows, HD), jnp.float32)
    return pl.pallas_call(
        functools.partial(attn_kernel, sizes, first_block, begin, end),
        grid=(rows // bq,),
        in_specs=[block] * (2 if begin else 5)
        + [pl.BlockSpec(kv.shape, lambda i: (0, 0)) for kv in kvs],
        out_specs=block if end else [block] * 3,
        out_shape=jax.ShapeDtypeStruct((rows, HD), jnp.bfloat16) if end else [f32] * 3,
        compiler_params=pltpu.CompilerParams(vmem_limit_bytes=28 << 20),
        cost_estimate=pl.CostEstimate(
            flops=8 * rows * keys * HD, bytes_accessed=keys * 512, transcendentals=rows * keys
        ),
    )(q, qm, *([] if begin else state), *kvs)


def local(tokens, w_qkv, qkv_scale, block_mask, w_out):
    nu, nb, nt = lax.axis_size("ulysses"), lax.axis_size("blk"), lax.axis_size("tensor")
    u, b, t = lax.axis_index("ulysses"), lax.axis_index("blk"), lax.axis_index("tensor")
    y, core = b // 2, b % 2
    half = tokens.shape[0] // 2
    quarter = half // 2
    pp = lax.ppermute
    offsets = jnp.array(OFFSETS, jnp.int32)

    def direct(value, axis, n):
        return [value] + [pp(value, axis, ring(n, s)) for s in (1, -1, 2)]

    where = jnp.concatenate([(t + offsets) % nt, core[None], (u - offsets) % nu])
    w = jnp.transpose(w_qkv, (1, 0, 2))
    hold = lax.optimization_barrier
    scale = qkv_scale * jnp.array([LOG2E / math.sqrt(HD), 1.0, 1.0], jnp.float32)[:, None]
    scale = jnp.repeat(scale.reshape(1, 6), HD, axis=1)

    ny = nb // 2
    groups = (u + offsets) % nu
    cores = jnp.stack([core, 1 - core])

    def block_id(yy, slot, group, odd):
        return (groups[group] * nb + 2 * (yy % ny) + cores[slot]) * 2 + odd

    early = [(g, 0) for g in range(3)]
    late = [(3, 0)] + [(g, 1) for g in range(4)]
    def ring_order(part):
        own = [(y, s) + g for s in (0, 1) for g in part]
        near = [(y + o, s) + g for o in (-1, 1) for s in (0, 1) for g in part]
        far = [(y + 2, s) + g for s in (0, 1) for g in part]
        return own, near, far

    early_ids, late_ids = ring_order(early), ring_order(late)
    keys = sum(early_ids, []) + sum(late_ids, [])
    key_ids = jnp.stack([block_id(*k) for k in keys])
    query_ids = jnp.stack(
        [block_id(y, s, g, odd) for s in (0, 1) for odd in (0, 1) for g in range(4)]
    )
    blocks = jnp.arange(block_mask.shape[1], dtype=jnp.int32)
    key_hot = (key_ids[:, None] == blocks[None, :]).astype(jnp.float32)
    query_hot = (query_ids[:, None] == blocks[None, :]).astype(jnp.float32)
    mask = lax.dynamic_index_in_dim(block_mask, core, 0, keepdims=False).astype(jnp.float32)
    live = query_hot @ mask @ key_hot.T > 0.5
    live = live | (query_ids[:, None] == key_ids[None, :])
    bias = jnp.where(live, 0.0, NEG).astype(jnp.bfloat16)
    bias = jnp.pad(bias, ((0, 0), (0, HD - bias.shape[1])))
    bias = jnp.repeat(bias, BLOCK, axis=0)

    a_own = jnp.concatenate(direct(tokens[:half], "tensor", nt), axis=1)
    b_own = jnp.concatenate(direct(tokens[half:], "ulysses", nu), axis=0)
    a_m = pp(a_own, "ulysses", ring(nu, 1))
    b_m = pp(b_own, "tensor", ring(nt, 1))
    a_p = pp(a_own, "ulysses", ring(nu, -1))
    b_p = pp(b_own, "tensor", ring(nt, -1))
    ah, bh = a_own.shape[0] // 2, b_own.shape[0] // 2
    done, part = project_stage(where, w, scale, [a_own], [b_own], (0,), None, None, False)
    done, bias, a_m = hold((done, bias, a_m))
    a0 = pp(a_m[:ah], "ulysses", ring(nu, 1))
    a1 = pp(a_p[ah:], "ulysses", ring(nu, -1))
    b0 = pp(b_m[:bh], "tensor", ring(nt, 1))
    b1 = pp(b_p[bh:], "tensor", ring(nt, -1))

    def swap(kv, give):
        got = pp(give, "blk", core_swap(nb))
        return got[:, :HD], jnp.concatenate([kv, got[:, HD:]], axis=0)

    def near_y(kv):
        return [pp(kv, "blk", y_ring(nb, s)) for s in (1, -1)]

    def far_y(kv_m, kv_p):
        h = kv_m.shape[0] // 2
        return [pp(kv_m[:h], "blk", y_ring(nb, 1)), pp(kv_p[h:], "blk", y_ring(nb, -1))]

    q1, kv1, give1 = project_stage(where, w, scale, [a_m, a_p], [], (), done, None, False)
    q1x, kv1 = swap(kv1, give1)
    part, kv1 = hold((part, kv1))
    part = project_part(where, w, [b_m, b_p], (1, 2), part)
    kv1_near = near_y(kv1)
    q2, kv2, give2 = project_stage(where, w, scale, [a0, a1], [b0, b1], (3, 3), None, part, True)
    give2, kv1_near = hold((give2, kv1_near))
    q2x, kv2 = swap(kv2, give2)
    kv1_far = far_y(*kv1_near)
    kv2_near = near_y(kv2)
    kv2_far = far_y(*kv2_near)

    q = jnp.concatenate([q1, q2, q1x, q2x], axis=0)
    state = attention(q, bias, [kv1] + kv1_near, (768,) * 3, 0, None, False)
    state = attention(q, bias, kv1_far + [kv2], (384, 384, 640), 18, state, False)
    state = attention(q, bias, kv2_near, (640, 640), 34, state, False)
    out = attention(q, bias, kv2_far, (640, 640), 54, state, True)

    out = out.reshape(2, 2, nu, half, HD)
    other = pp(out[1], "blk", core_swap(nb))
    mine = out[0]
    first = jnp.where(core == 0, mine, other)
    second = jnp.where(core == 0, other, mine)
    heads = jnp.concatenate([first, second], axis=-1)
    heads = [heads[:, g].reshape(2 * half, 2 * HD) for g in range(nu)]
    arrived = [heads[0]] + [
        pp(heads[i], "ulysses", ring(nu, OFFSETS[i])) for i in range(1, nu)
    ]
    w_o = load_columns(where, w_out, heads[0])
    bf = jnp.bfloat16
    far_0, far_1 = out_project(where, arrived, w_o, (3,), bf, 2)
    rows = 2 * half
    hr = rows // 2
    far_m = pp(far_0, "tensor", ring(nt, 1))
    far_p = pp(far_1, "tensor", ring(nt, -1))
    to_m, to_p = out_project(where, arrived, w_o, (1, 2), jnp.float32, 1)
    to_p = jnp.concatenate([to_p[:hr] + far_m.astype(jnp.float32), to_p[hr:]], axis=0).astype(bf)
    to_m = jnp.concatenate([to_m[:hr], to_m[hr:] + far_p.astype(jnp.float32)], axis=0).astype(bf)
    from_m = pp(to_p, "tensor", ring(nt, 1))
    from_p = pp(to_m, "tensor", ring(nt, -1))
    (own,) = out_project(where, arrived, w_o, (0,), jnp.float32, 1)
    return (own + from_m.astype(jnp.float32) + from_p.astype(jnp.float32)).astype(bf)


def solution(mesh):
    return jax.shard_map(
        local,
        mesh=mesh,
        in_specs=(
            P(("ulysses", "blk"), "tensor"),
            P(None, None, ("ulysses", "tensor")),
            P(None, ("ulysses", "tensor")),
            P(("ulysses", "tensor"), None, None),
            P(None, "tensor", None),
        ),
        out_specs=P(("ulysses", "blk"), "tensor"),
        check_vma=False,
    )
```

```python
import functools
import math

import jax
import jax.numpy as jnp
from jax import lax
from jax.experimental import pallas as pl
from jax.experimental.pallas import tpu as pltpu
from jax.sharding import PartitionSpec as P

HD = 128
BLOCK = 128
NEG = -1e30
LOG2E = 1.4426950408889634
OFFSETS = (0, -1, 1, 2)
CONTRACT_LAST = (((1,), (1,)), ((), ()))


def ring(n, step):
    return [(i, (i + step) % n) for i in range(n)]


def y_ring(n, step):
    return [(i, (i + 2 * step) % n) for i in range(n)]


def core_swap(n):
    return [(i, i ^ 1) for i in range(n)]


def emit_heads(acc, scale_ref, core, q_ref, kv_ref, give_ref):
    scaled = (acc * scale_ref[...]).astype(jnp.bfloat16)
    heads = [[scaled[:, c * 256 + h * HD : c * 256 + (h + 1) * HD] for c in range(3)] for h in (0, 1)]
    is_first = core == 0

    @pl.when(is_first)
    def _():
        q_ref[...] = heads[0][0]
        kv_ref[...] = jnp.concatenate(heads[0][1:], axis=1)
        give_ref[...] = jnp.concatenate(heads[1], axis=1)

    @pl.when(jnp.logical_not(is_first))
    def _():
        q_ref[...] = heads[1][0]
        kv_ref[...] = jnp.concatenate(heads[1][1:], axis=1)
        give_ref[...] = jnp.concatenate(heads[0], axis=1)


def heads_shape(rows):
    return [jax.ShapeDtypeStruct((rows, n * HD), jnp.bfloat16) for n in (1, 2, 3)]


def load_kernel(where_ref, x_ref, hbm, o_ref, sems):
    width = o_ref.shape[3]
    copies = []
    for i in range(4):
        cols = pl.ds(pl.multiple_of(where_ref[i] * width, width), width)
        copies.append(pltpu.make_async_copy(hbm.at[:, :, cols], o_ref.at[i], sems.at[i]))
        copies[-1].start()
    for copy in copies:
        copy.wait()


def load_columns(where, w, x):
    return pl.pallas_call(
        load_kernel,
        in_specs=[pl.BlockSpec(memory_space=pltpu.SMEM), VM, pl.BlockSpec(memory_space=pltpu.HBM)],
        out_specs=VM,
        out_shape=jax.ShapeDtypeStruct((4,) + w.shape[:2] + (w.shape[2] // 4,), w.dtype),
        scratch_shapes=[pltpu.SemaphoreType.DMA((4,))],
        compiler_params=pltpu.CompilerParams(vmem_limit_bytes=40 << 20),
        cost_estimate=pl.CostEstimate(flops=0, bytes_accessed=w.size * 4, transcendentals=0),
    )(where, x, w)


def stage_kernel(n_a, b_slices, n_done, has_part, emit_all, where_ref, w_ref, scale_ref, *refs):
    a_refs, refs = refs[:n_a], refs[n_a:]
    b_refs, refs = refs[: len(b_slices)], refs[len(b_slices) :]
    done_refs, refs = refs[:n_done], refs[n_done:]
    part_refs, refs = refs[:has_part], refs[has_part:]
    outs, acc_ref = refs[:-1], refs[-1]
    feat = w_ref.shape[1] // 4
    na = sum(r.shape[0] for r in a_refs)
    fresh = not has_part
    for i in range(4):
        at = pl.ds(pl.multiple_of(where_ref[i] * feat, feat), feat)
        x = [r[:, i * feat : (i + 1) * feat] for r in a_refs]
        x += [r[...] for r, s in zip(b_refs, b_slices) if s == i]
        with_b = len(x) > n_a
        x = jnp.concatenate(x, axis=0) if len(x) > 1 else x[0]
        for c in range(3):
            cols = slice(c * 256, (c + 1) * 256)
            d = jnp.dot(x, w_ref[c, at, :], preferred_element_type=jnp.float32)
            acc_ref[:na, cols] = d[:na] if i == 0 else acc_ref[:na, cols] + d[:na]
            if with_b:
                first = i == min(b_slices)
                before = None if first and fresh else part_refs[0][:, cols] if first else acc_ref[na:, cols]
                acc_ref[na:, cols] = d[na:] if before is None else before + d[na:]
    if not emit_all and not n_done:
        outs[0][...] = acc_ref[:na]
        outs[1][...] = acc_ref[na:]
        return
    rows = acc_ref[...] if emit_all else acc_ref[:na]
    if n_done:
        rows = jnp.concatenate([done_refs[0][...], rows], axis=0)
    emit_heads(rows, scale_ref, where_ref[4], *outs[:3])
    if not emit_all and b_slices:
        outs[3][...] = acc_ref[na:]


def part_kernel(b_slices, where_ref, w_ref, part_ref, *refs):
    b_refs, o_ref = refs[:-1], refs[-1]
    feat = w_ref.shape[1] // 4
    for c in range(3):
        cols = slice(c * 256, (c + 1) * 256)
        d = part_ref[:, cols]
        for i, b_ref in zip(b_slices, b_refs):
            at = pl.ds(pl.multiple_of(where_ref[i] * feat, feat), feat)
            d = d + jnp.dot(b_ref[...], w_ref[c, at, :], preferred_element_type=jnp.float32)
        o_ref[:, cols] = d


def project_part(where, w, b_parts, b_slices, part):
    return pl.pallas_call(
        functools.partial(part_kernel, b_slices),
        in_specs=FIXED[:2] + [VM] * (1 + len(b_parts)),
        out_specs=VM,
        out_shape=jax.ShapeDtypeStruct(part.shape, part.dtype),
        compiler_params=pltpu.CompilerParams(vmem_limit_bytes=16 << 20),
        cost_estimate=pl.CostEstimate(
            flops=2 * 768 * sum(x.size for x in b_parts), bytes_accessed=w.size, transcendentals=0
        ),
    )(where, w, part, *b_parts)


VM = pl.BlockSpec(memory_space=pltpu.VMEM)
FIXED = [pl.BlockSpec(memory_space=pltpu.SMEM), VM, VM]


def project_stage(where, w, scale, a_parts, b_parts, b_slices, done, part, emit_all):
    feat = w.shape[1] // 4
    na = sum(x.shape[0] for x in a_parts)
    nb = part.shape[0] if part is not None else b_parts[0].shape[0] if b_parts else 0
    f32 = lambda n: jax.ShapeDtypeStruct((n, 768), jnp.float32)
    if emit_all:
        shapes = heads_shape(na + nb)
    elif done is not None:
        shapes = heads_shape(done.shape[0] + na) + ([f32(nb)] if b_parts else [])
    else:
        shapes = [f32(na), f32(nb)]
    extra = [x for x in (done, part) if x is not None]
    return pl.pallas_call(
        functools.partial(
            stage_kernel, len(a_parts), b_slices, int(done is not None), int(part is not None), emit_all
        ),
        in_specs=FIXED + [VM] * (len(a_parts) + len(b_parts) + len(extra)),
        out_specs=[VM] * len(shapes),
        out_shape=shapes,
        scratch_shapes=[pltpu.VMEM((na + nb, 768), jnp.float32)],
        compiler_params=pltpu.CompilerParams(vmem_limit_bytes=16 << 20),
        cost_estimate=pl.CostEstimate(
            flops=2 * 768 * feat * (4 * na + sum(x.shape[0] for x in b_parts)),
            bytes_accessed=w.size * 2,
            transcendentals=0,
        ),
    )(where, w, scale, *a_parts, *b_parts, *extra)


def out_kernel(places, where_ref, *refs):
    xs, w_ref, outs = refs[:4], refs[4], refs[5:]
    per_place = len(outs) // len(places)
    for n, place in enumerate(places):
        d = sum(
            jnp.dot(x_ref[...], w_ref[place, where_ref[5 + i]], preferred_element_type=jnp.float32)
            for i, x_ref in enumerate(xs)
        )
        at = 0
        for o_ref in outs[n * per_place : (n + 1) * per_place]:
            o_ref[...] = d[at : at + o_ref.shape[0]].astype(o_ref.dtype)
            at += o_ref.shape[0]


def out_project(where, xs, w, places, dtype, pieces):
    rows, cols = xs[0].shape[0], w.shape[3]
    n = len(places) * pieces
    return pl.pallas_call(
        functools.partial(out_kernel, places),
        in_specs=[pl.BlockSpec(memory_space=pltpu.SMEM)] + [VM] * 5,
        out_specs=[VM] * n,
        out_shape=[jax.ShapeDtypeStruct((rows // pieces, cols), dtype)] * n,
        compiler_params=pltpu.CompilerParams(vmem_limit_bytes=16 << 20),
        cost_estimate=pl.CostEstimate(
            flops=2 * len(places) * rows * 1024 * cols, bytes_accessed=n * 4 * rows * cols, transcendentals=0
        ),
    )(where, *xs, w)


def attn_kernel(sizes, first_block, begin, end, q_ref, qm_ref, *refs):
    if not begin:
        state_refs, refs = refs[:3], refs[3:]
    kv_refs, outs = refs[: len(sizes)], refs[len(sizes) :]
    rows = q_ref.shape[0]
    q = jnp.concatenate([q_ref[...], qm_ref[...]], axis=1)
    tiles = []
    for kv_ref, bk in zip(kv_refs, sizes):
        j = 0
        for size in bk * (kv_ref.shape[0] // sum(bk)):
            tiles.append((kv_ref, slice(j, j + size), size, first_block))
            first_block += size // BLOCK
            j += size

    def score(tile):
        kv_ref, at, bk, block = tile
        lane = lax.broadcasted_iota(jnp.int32, (bk, HD), 1)
        inner = lax.broadcasted_iota(jnp.int32, (bk, HD), 0) // BLOCK
        onehot = (lane == inner + block).astype(jnp.float32).astype(jnp.bfloat16)
        k = jnp.concatenate([kv_ref[at, :HD], onehot], axis=1)
        return lax.dot_general(q, k, CONTRACT_LAST, preferred_element_type=jnp.float32)

    s = score(tiles[0])
    for i, (kv_ref, at, bk, _) in enumerate(tiles):
        s_next = score(tiles[i + 1]) if i + 1 < len(tiles) else None
        top = jnp.max(s, axis=1, keepdims=True)
        v = jnp.concatenate([kv_ref[at, HD:], jnp.ones((bk, HD), jnp.bfloat16)], axis=1)
        fresh = begin and i == 0
        if fresh:
            high = jnp.broadcast_to(top, (rows, HD))
        else:
            if i == 0:
                old = state_refs[2][...]
                acc = jnp.concatenate([state_refs[0][...], state_refs[1][...]], axis=1)
            else:
                old = high
            high = jnp.maximum(old, top)
        p = jnp.exp2(s - jnp.concatenate([high] * (bk // HD), axis=1)).astype(jnp.bfloat16)
        d = jnp.dot(p, v, preferred_element_type=jnp.float32)
        if fresh:
            acc = d
        else:
            factor = jnp.exp2(old - high)
            acc = acc * jnp.concatenate([factor, factor], axis=1) + d
        s = s_next
    if end:
        outs[0][...] = (acc[:, :HD] / acc[:, HD:]).astype(jnp.bfloat16)
    else:
        outs[0][...] = acc[:, :HD]
        outs[1][...] = acc[:, HD:]
        outs[2][...] = high


def attention(q, qm, kvs, sizes, first_block, state, end, bq=1024):
    rows = q.shape[0]
    keys = sum(kv.shape[0] for kv in kvs)
    begin = state is None
    block = pl.BlockSpec((bq, HD), lambda i: (i, 0))
    f32 = jax.ShapeDtypeStruct((rows, HD), jnp.float32)
    return pl.pallas_call(
        functools.partial(attn_kernel, sizes, first_block, begin, end),
        grid=(rows // bq,),
        in_specs=[block] * (2 if begin else 5)
        + [pl.BlockSpec(kv.shape, lambda i: (0, 0)) for kv in kvs],
        out_specs=block if end else [block] * 3,
        out_shape=jax.ShapeDtypeStruct((rows, HD), jnp.bfloat16) if end else [f32] * 3,
        compiler_params=pltpu.CompilerParams(vmem_limit_bytes=28 << 20),
        cost_estimate=pl.CostEstimate(
            flops=8 * rows * keys * HD, bytes_accessed=keys * 512, transcendentals=rows * keys
        ),
    )(q, qm, *([] if begin else state), *kvs)


def local(tokens, w_qkv, qkv_scale, block_mask, w_out):
    nu, nb, nt = lax.axis_size("ulysses"), lax.axis_size("blk"), lax.axis_size("tensor")
    u, b, t = lax.axis_index("ulysses"), lax.axis_index("blk"), lax.axis_index("tensor")
    y, core = b // 2, b % 2
    half = tokens.shape[0] // 2
    quarter = half // 2
    pp = lax.ppermute
    offsets = jnp.array(OFFSETS, jnp.int32)

    def direct(value, axis, n):
        return [value] + [pp(value, axis, ring(n, s)) for s in (1, -1, 2)]

    where = jnp.concatenate([(t + offsets) % nt, core[None], (u - offsets) % nu])
    w = jnp.transpose(w_qkv, (1, 0, 2))
    hold = lax.optimization_barrier
    scale = qkv_scale * jnp.array([LOG2E / math.sqrt(HD), 1.0, 1.0], jnp.float32)[:, None]
    scale = jnp.repeat(scale.reshape(1, 6), HD, axis=1)

    ny = nb // 2
    groups = (u + offsets) % nu
    cores = jnp.stack([core, 1 - core])

    def block_id(yy, slot, group, odd):
        return (groups[group] * nb + 2 * (yy % ny) + cores[slot]) * 2 + odd

    early = [(g, 0) for g in range(3)]
    late = [(3, 0)] + [(g, 1) for g in range(4)]
    def ring_order(part):
        own = [(y, s) + g for s in (0, 1) for g in part]
        near = [(y + o, s) + g for o in (-1, 1) for s in (0, 1) for g in part]
        far = [(y + 2, s) + g for s in (0, 1) for g in part]
        return own, near, far

    early_ids, late_ids = ring_order(early), ring_order(late)
    keys = early_ids[0] + early_ids[1] + late_ids[0] + late_ids[1] + early_ids[2] + late_ids[2]
    key_ids = jnp.stack([block_id(*k) for k in keys])
    query_ids = jnp.stack(
        [block_id(y, s, g, odd) for s in (0, 1) for odd in (0, 1) for g in range(4)]
    )
    blocks = jnp.arange(block_mask.shape[1], dtype=jnp.int32)
    key_hot = (key_ids[:, None] == blocks[None, :]).astype(jnp.float32)
    query_hot = (query_ids[:, None] == blocks[None, :]).astype(jnp.float32)
    mask = lax.dynamic_index_in_dim(block_mask, core, 0, keepdims=False).astype(jnp.float32)
    live = query_hot @ mask @ key_hot.T > 0.5
    live = live | (query_ids[:, None] == key_ids[None, :])
    bias = jnp.where(live, 0.0, NEG).astype(jnp.bfloat16)
    bias = jnp.pad(bias, ((0, 0), (0, HD - bias.shape[1])))
    bias = jnp.repeat(bias, BLOCK, axis=0)

    a_own = jnp.concatenate(direct(tokens[:half], "tensor", nt), axis=1)
    b_own = jnp.concatenate(direct(tokens[half:], "ulysses", nu), axis=0)
    a_m = pp(a_own, "ulysses", ring(nu, 1))
    b_m = pp(b_own, "tensor", ring(nt, 1))
    a_p = pp(a_own, "ulysses", ring(nu, -1))
    b_p = pp(b_own, "tensor", ring(nt, -1))
    ah, bh = a_own.shape[0] // 2, b_own.shape[0] // 2
    done, part = project_stage(where, w, scale, [a_own], [b_own], (0,), None, None, False)
    done, bias, a_m = hold((done, bias, a_m))
    a0 = pp(a_m[:ah], "ulysses", ring(nu, 1))
    a1 = pp(a_p[ah:], "ulysses", ring(nu, -1))
    b0 = pp(b_m[:bh], "tensor", ring(nt, 1))
    b1 = pp(b_p[bh:], "tensor", ring(nt, -1))

    def swap(kv, give):
        got = pp(give, "blk", core_swap(nb))
        return got[:, :HD], jnp.concatenate([kv, got[:, HD:]], axis=0)

    def near_y(kv):
        return [pp(kv, "blk", y_ring(nb, s)) for s in (1, -1)]

    def far_y(kv_m, kv_p):
        h = kv_m.shape[0] // 2
        return [pp(kv_m[:h], "blk", y_ring(nb, 1)), pp(kv_p[h:], "blk", y_ring(nb, -1))]

    q1, kv1, give1 = project_stage(where, w, scale, [a_m, a_p], [], (), done, None, False)
    q1x, kv1 = swap(kv1, give1)
    part, kv1 = hold((part, kv1))
    part = project_part(where, w, [b_m, b_p], (1, 2), part)
    kv1_near = near_y(kv1)
    q2, kv2, give2 = project_stage(where, w, scale, [a0, a1], [b0, b1], (3, 3), None, part, True)
    give2, kv1_near = hold((give2, kv1_near))
    q2x, kv2 = swap(kv2, give2)
    kv2_near = near_y(kv2)
    q = jnp.concatenate([q1, q2, q1x, q2x], axis=0)
    q, kv1_near = hold((q, kv1_near))
    kv1_far = far_y(*kv1_near)
    kv2_far = far_y(*kv2_near)

    big = (512, 512, 256)
    state = attention(q, bias, [kv1] + kv1_near + [kv2], ((768,),) * 3 + (big,), 0, None, False)
    state = attention(q, bias, kv2_near + kv1_far, (big, big, (384,), (384,)), 28, state, False)
    out = attention(q, bias, kv2_far, ((384, 256),) * 2, 54, state, True)

    out = out.reshape(2, 2, nu, half, HD)
    other = pp(out[1], "blk", core_swap(nb))
    mine = out[0]
    first = jnp.where(core == 0, mine, other)
    second = jnp.where(core == 0, other, mine)
    heads = jnp.concatenate([first, second], axis=-1)
    heads = [heads[:, g].reshape(2 * half, 2 * HD) for g in range(nu)]
    arrived = [heads[0]] + [
        pp(heads[i], "ulysses", ring(nu, OFFSETS[i])) for i in range(1, nu)
    ]
    w_o = load_columns(where, w_out, heads[0])
    bf = jnp.bfloat16
    far_0, far_1 = out_project(where, arrived, w_o, (3,), bf, 2)
    rows = 2 * half
    hr = rows // 2
    far_m = pp(far_0, "tensor", ring(nt, 1))
    far_p = pp(far_1, "tensor", ring(nt, -1))
    to_m, to_p = out_project(where, arrived, w_o, (1, 2), jnp.float32, 1)
    to_p = jnp.concatenate([to_p[:hr] + far_m.astype(jnp.float32), to_p[hr:]], axis=0).astype(bf)
    to_m = jnp.concatenate([to_m[:hr], to_m[hr:] + far_p.astype(jnp.float32)], axis=0).astype(bf)
    from_m = pp(to_p, "tensor", ring(nt, 1))
    from_p = pp(to_m, "tensor", ring(nt, -1))
    (own,) = out_project(where, arrived, w_o, (0,), jnp.float32, 1)
    return (own + from_m.astype(jnp.float32) + from_p.astype(jnp.float32)).astype(bf)


def solution(mesh):
    return jax.shard_map(
        local,
        mesh=mesh,
        in_specs=(
            P(("ulysses", "blk"), "tensor"),
            P(None, None, ("ulysses", "tensor")),
            P(None, ("ulysses", "tensor")),
            P(("ulysses", "tensor"), None, None),
            P(None, "tensor", None),
        ),
        out_specs=P(("ulysses", "blk"), "tensor"),
        check_vma=False,
    )
```

```python
import functools
import math

import jax
import jax.numpy as jnp
from jax import lax
from jax.experimental import pallas as pl
from jax.experimental.pallas import tpu as pltpu
from jax.sharding import PartitionSpec as P

HD = 128
BLOCK = 128
NEG = -1e30
LOG2E = 1.4426950408889634
OFFSETS = (0, -1, 1, 2)
CONTRACT_LAST = (((1,), (1,)), ((), ()))


def ring(n, step):
    return [(i, (i + step) % n) for i in range(n)]


def y_ring(n, step):
    return [(i, (i + 2 * step) % n) for i in range(n)]


def core_swap(n):
    return [(i, i ^ 1) for i in range(n)]


def emit_heads(acc, scale_ref, core, q_ref, kv_ref, give_ref):
    scaled = (acc * scale_ref[...]).astype(jnp.bfloat16)
    heads = [[scaled[:, c * 256 + h * HD : c * 256 + (h + 1) * HD] for c in range(3)] for h in (0, 1)]
    is_first = core == 0

    @pl.when(is_first)
    def _():
        q_ref[...] = heads[0][0]
        kv_ref[...] = jnp.concatenate(heads[0][1:], axis=1)
        give_ref[...] = jnp.concatenate(heads[1], axis=1)

    @pl.when(jnp.logical_not(is_first))
    def _():
        q_ref[...] = heads[1][0]
        kv_ref[...] = jnp.concatenate(heads[1][1:], axis=1)
        give_ref[...] = jnp.concatenate(heads[0], axis=1)


def heads_shape(rows):
    return [jax.ShapeDtypeStruct((rows, n * HD), jnp.bfloat16) for n in (1, 2, 3)]


def load_kernel(where_ref, x_ref, hbm, o_ref, sems):
    width = o_ref.shape[3]
    copies = []
    for i in range(4):
        cols = pl.ds(pl.multiple_of(where_ref[i] * width, width), width)
        copies.append(pltpu.make_async_copy(hbm.at[:, :, cols], o_ref.at[i], sems.at[i]))
        copies[-1].start()
    for copy in copies:
        copy.wait()


def load_columns(where, w, x):
    return pl.pallas_call(
        load_kernel,
        in_specs=[pl.BlockSpec(memory_space=pltpu.SMEM), VM, pl.BlockSpec(memory_space=pltpu.HBM)],
        out_specs=VM,
        out_shape=jax.ShapeDtypeStruct((4,) + w.shape[:2] + (w.shape[2] // 4,), w.dtype),
        scratch_shapes=[pltpu.SemaphoreType.DMA((4,))],
        compiler_params=pltpu.CompilerParams(vmem_limit_bytes=40 << 20),
        cost_estimate=pl.CostEstimate(flops=0, bytes_accessed=w.size * 4, transcendentals=0),
    )(where, x, w)


def stage_kernel(n_a, b_slices, n_done, has_part, emit_all, where_ref, w_ref, scale_ref, *refs):
    a_refs, refs = refs[:n_a], refs[n_a:]
    b_refs, refs = refs[: len(b_slices)], refs[len(b_slices) :]
    done_refs, refs = refs[:n_done], refs[n_done:]
    part_refs, refs = refs[:has_part], refs[has_part:]
    outs, acc_ref = refs[:-1], refs[-1]
    feat = w_ref.shape[1] // 4
    na = sum(r.shape[0] for r in a_refs)
    fresh = not has_part
    for i in range(4):
        at = pl.ds(pl.multiple_of(where_ref[i] * feat, feat), feat)
        x = [r[:, i * feat : (i + 1) * feat] for r in a_refs]
        x += [r[...] for r, s in zip(b_refs, b_slices) if s == i]
        with_b = len(x) > n_a
        x = jnp.concatenate(x, axis=0) if len(x) > 1 else x[0]
        for c in range(3):
            cols = slice(c * 256, (c + 1) * 256)
            d = jnp.dot(x, w_ref[c, at, :], preferred_element_type=jnp.float32)
            acc_ref[:na, cols] = d[:na] if i == 0 else acc_ref[:na, cols] + d[:na]
            if with_b:
                first = i == min(b_slices)
                before = None if first and fresh else part_refs[0][:, cols] if first else acc_ref[na:, cols]
                acc_ref[na:, cols] = d[na:] if before is None else before + d[na:]
    if not emit_all and not n_done:
        outs[0][...] = acc_ref[:na]
        outs[1][...] = acc_ref[na:]
        return
    rows = acc_ref[...] if emit_all else acc_ref[:na]
    if n_done:
        rows = jnp.concatenate([done_refs[0][...], rows], axis=0)
    emit_heads(rows, scale_ref, where_ref[4], *outs[:3])
    if not emit_all and b_slices:
        outs[3][...] = acc_ref[na:]


def part_kernel(b_slices, where_ref, w_ref, part_ref, *refs):
    b_refs, o_ref = refs[:-1], refs[-1]
    feat = w_ref.shape[1] // 4
    for c in range(3):
        cols = slice(c * 256, (c + 1) * 256)
        d = part_ref[:, cols]
        for i, b_ref in zip(b_slices, b_refs):
            at = pl.ds(pl.multiple_of(where_ref[i] * feat, feat), feat)
            d = d + jnp.dot(b_ref[...], w_ref[c, at, :], preferred_element_type=jnp.float32)
        o_ref[:, cols] = d


def project_part(where, w, b_parts, b_slices, part):
    return pl.pallas_call(
        functools.partial(part_kernel, b_slices),
        in_specs=FIXED[:2] + [VM] * (1 + len(b_parts)),
        out_specs=VM,
        out_shape=jax.ShapeDtypeStruct(part.shape, part.dtype),
        compiler_params=pltpu.CompilerParams(vmem_limit_bytes=16 << 20),
        cost_estimate=pl.CostEstimate(
            flops=2 * 768 * sum(x.size for x in b_parts), bytes_accessed=w.size, transcendentals=0
        ),
    )(where, w, part, *b_parts)


VM = pl.BlockSpec(memory_space=pltpu.VMEM)
FIXED = [pl.BlockSpec(memory_space=pltpu.SMEM), VM, VM]


def project_stage(where, w, scale, a_parts, b_parts, b_slices, done, part, emit_all):
    feat = w.shape[1] // 4
    na = sum(x.shape[0] for x in a_parts)
    nb = part.shape[0] if part is not None else b_parts[0].shape[0] if b_parts else 0
    f32 = lambda n: jax.ShapeDtypeStruct((n, 768), jnp.float32)
    if emit_all:
        shapes = heads_shape(na + nb)
    elif done is not None:
        shapes = heads_shape(done.shape[0] + na) + ([f32(nb)] if b_parts else [])
    else:
        shapes = [f32(na), f32(nb)]
    extra = [x for x in (done, part) if x is not None]
    return pl.pallas_call(
        functools.partial(
            stage_kernel, len(a_parts), b_slices, int(done is not None), int(part is not None), emit_all
        ),
        in_specs=FIXED + [VM] * (len(a_parts) + len(b_parts) + len(extra)),
        out_specs=[VM] * len(shapes),
        out_shape=shapes,
        scratch_shapes=[pltpu.VMEM((na + nb, 768), jnp.float32)],
        compiler_params=pltpu.CompilerParams(vmem_limit_bytes=16 << 20),
        cost_estimate=pl.CostEstimate(
            flops=2 * 768 * feat * (4 * na + sum(x.shape[0] for x in b_parts)),
            bytes_accessed=w.size * 2,
            transcendentals=0,
        ),
    )(where, w, scale, *a_parts, *b_parts, *extra)


def out_kernel(places, where_ref, *refs):
    xs, w_ref, outs = refs[:4], refs[4], refs[5:]
    per_place = len(outs) // len(places)
    for n, place in enumerate(places):
        d = sum(
            jnp.dot(x_ref[...], w_ref[place, where_ref[5 + i]], preferred_element_type=jnp.float32)
            for i, x_ref in enumerate(xs)
        )
        at = 0
        for o_ref in outs[n * per_place : (n + 1) * per_place]:
            o_ref[...] = d[at : at + o_ref.shape[0]].astype(o_ref.dtype)
            at += o_ref.shape[0]


def out_project(where, xs, w, places, dtype, pieces):
    rows, cols = xs[0].shape[0], w.shape[3]
    n = len(places) * pieces
    return pl.pallas_call(
        functools.partial(out_kernel, places),
        in_specs=[pl.BlockSpec(memory_space=pltpu.SMEM)] + [VM] * 5,
        out_specs=[VM] * n,
        out_shape=[jax.ShapeDtypeStruct((rows // pieces, cols), dtype)] * n,
        compiler_params=pltpu.CompilerParams(vmem_limit_bytes=16 << 20),
        cost_estimate=pl.CostEstimate(
            flops=2 * len(places) * rows * 1024 * cols, bytes_accessed=n * 4 * rows * cols, transcendentals=0
        ),
    )(where, *xs, w)


def attn_kernel(sizes, first_block, begin, end, q_ref, qm_ref, *refs):
    if not begin:
        state_refs, refs = refs[:3], refs[3:]
    kv_refs, outs = refs[: len(sizes)], refs[len(sizes) :]
    rows = q_ref.shape[0]
    q = jnp.concatenate([q_ref[...], qm_ref[...]], axis=1)
    tiles = []
    for kv_ref, bk in zip(kv_refs, sizes):
        j = 0
        for size in bk * (kv_ref.shape[0] // sum(bk)):
            tiles.append((kv_ref, slice(j, j + size), size, first_block))
            first_block += size // BLOCK
            j += size

    def score(tile):
        kv_ref, at, bk, block = tile
        lane = lax.broadcasted_iota(jnp.int32, (bk, HD), 1)
        inner = lax.broadcasted_iota(jnp.int32, (bk, HD), 0) // BLOCK
        onehot = (lane == inner + block).astype(jnp.float32).astype(jnp.bfloat16)
        k = jnp.concatenate([kv_ref[at, :HD], onehot], axis=1)
        return lax.dot_general(q, k, CONTRACT_LAST, preferred_element_type=jnp.float32)

    s = score(tiles[0])
    for i, (kv_ref, at, bk, _) in enumerate(tiles):
        s_next = score(tiles[i + 1]) if i + 1 < len(tiles) else None
        top = jnp.max(s, axis=1, keepdims=True)
        v = jnp.concatenate([kv_ref[at, HD:], jnp.ones((bk, HD), jnp.bfloat16)], axis=1)
        fresh = begin and i == 0
        if fresh:
            high = jnp.broadcast_to(top, (rows, HD))
        else:
            if i == 0:
                old = state_refs[2][...]
                acc = jnp.concatenate([state_refs[0][...], state_refs[1][...]], axis=1)
            else:
                old = high
            high = jnp.maximum(old, top)
        p = jnp.exp2(s - jnp.concatenate([high] * (bk // HD), axis=1)).astype(jnp.bfloat16)
        d = jnp.dot(p, v, preferred_element_type=jnp.float32)
        if fresh:
            acc = d
        else:
            factor = jnp.exp2(old - high)
            acc = acc * jnp.concatenate([factor, factor], axis=1) + d
        s = s_next
    if end:
        outs[0][...] = (acc[:, :HD] / acc[:, HD:]).astype(jnp.bfloat16)
    else:
        outs[0][...] = acc[:, :HD]
        outs[1][...] = acc[:, HD:]
        outs[2][...] = high


def attention(q, qm, kvs, sizes, first_block, state, end, bq=1024):
    rows = q.shape[0]
    keys = sum(kv.shape[0] for kv in kvs)
    begin = state is None
    block = pl.BlockSpec((bq, HD), lambda i: (i, 0))
    f32 = jax.ShapeDtypeStruct((rows, HD), jnp.float32)
    return pl.pallas_call(
        functools.partial(attn_kernel, sizes, first_block, begin, end),
        grid=(rows // bq,),
        in_specs=[block] * (2 if begin else 5)
        + [pl.BlockSpec(kv.shape, lambda i: (0, 0)) for kv in kvs],
        out_specs=block if end else [block] * 3,
        out_shape=jax.ShapeDtypeStruct((rows, HD), jnp.bfloat16) if end else [f32] * 3,
        compiler_params=pltpu.CompilerParams(vmem_limit_bytes=28 << 20),
        cost_estimate=pl.CostEstimate(
            flops=8 * rows * keys * HD, bytes_accessed=keys * 512, transcendentals=rows * keys
        ),
    )(q, qm, *([] if begin else state), *kvs)


def local(tokens, w_qkv, qkv_scale, block_mask, w_out):
    nu, nb, nt = lax.axis_size("ulysses"), lax.axis_size("blk"), lax.axis_size("tensor")
    u, b, t = lax.axis_index("ulysses"), lax.axis_index("blk"), lax.axis_index("tensor")
    y, core = b // 2, b % 2
    half = tokens.shape[0] // 2
    quarter = half // 2
    pp = lax.ppermute
    offsets = jnp.array(OFFSETS, jnp.int32)

    def direct(value, axis, n):
        return [value] + [pp(value, axis, ring(n, s)) for s in (1, -1, 2)]

    where = jnp.concatenate([(t + offsets) % nt, core[None], (u - offsets) % nu])
    w = jnp.transpose(w_qkv, (1, 0, 2))
    hold = lax.optimization_barrier
    scale = qkv_scale * jnp.array([LOG2E / math.sqrt(HD), 1.0, 1.0], jnp.float32)[:, None]
    scale = jnp.repeat(scale.reshape(1, 6), HD, axis=1)

    ny = nb // 2
    groups = (u + offsets) % nu
    cores = jnp.stack([core, 1 - core])

    def block_id(yy, slot, group, odd):
        return (groups[group] * nb + 2 * (yy % ny) + cores[slot]) * 2 + odd

    early = [(g, 0) for g in range(3)]
    late = [(3, 0)] + [(g, 1) for g in range(4)]
    def ring_order(part):
        own = [(y, s) + g for s in (0, 1) for g in part]
        near = [(y + o, s) + g for o in (-1, 1) for s in (0, 1) for g in part]
        far = [(y + 2, s) + g for s in (0, 1) for g in part]
        return own, near, far

    early_ids, late_ids = ring_order(early), ring_order(late)
    keys = early_ids[0] + early_ids[1] + late_ids[0] + late_ids[1] + early_ids[2] + late_ids[2]
    key_ids = jnp.stack([block_id(*k) for k in keys])
    query_ids = jnp.stack(
        [block_id(y, s, g, odd) for s in (0, 1) for odd in (0, 1) for g in range(4)]
    )
    blocks = jnp.arange(block_mask.shape[1], dtype=jnp.int32)
    key_hot = (key_ids[:, None] == blocks[None, :]).astype(jnp.float32)
    query_hot = (query_ids[:, None] == blocks[None, :]).astype(jnp.float32)
    mask = lax.dynamic_index_in_dim(block_mask, core, 0, keepdims=False).astype(jnp.float32)
    live = query_hot @ mask @ key_hot.T > 0.5
    live = live | (query_ids[:, None] == key_ids[None, :])
    bias = jnp.where(live, 0.0, NEG).astype(jnp.bfloat16)
    bias = jnp.pad(bias, ((0, 0), (0, HD - bias.shape[1])))
    bias = jnp.repeat(bias, BLOCK, axis=0)

    a_own = jnp.concatenate(direct(tokens[:half], "tensor", nt), axis=1)
    b_own = jnp.concatenate(direct(tokens[half:], "ulysses", nu), axis=0)
    a_m = pp(a_own, "ulysses", ring(nu, 1))
    b_m = pp(b_own, "tensor", ring(nt, 1))
    a_p = pp(a_own, "ulysses", ring(nu, -1))
    b_p = pp(b_own, "tensor", ring(nt, -1))
    ah, bh = a_own.shape[0] // 2, b_own.shape[0] // 2
    done, part = project_stage(where, w, scale, [a_own], [b_own], (0,), None, None, False)
    done, bias, a_m = hold((done, bias, a_m))
    a0 = pp(a_m[:ah], "ulysses", ring(nu, 1))
    a1 = pp(a_p[ah:], "ulysses", ring(nu, -1))
    b0 = pp(b_m[:bh], "tensor", ring(nt, 1))
    b1 = pp(b_p[bh:], "tensor", ring(nt, -1))

    def swap(kv, give):
        got = pp(give, "blk", core_swap(nb))
        return got[:, :HD], jnp.concatenate([kv, got[:, HD:]], axis=0)

    def near_y(kv):
        return [pp(kv, "blk", y_ring(nb, s)) for s in (1, -1)]

    def far_y(kv_m, kv_p):
        h = kv_m.shape[0] // 2
        return [pp(kv_m[:h], "blk", y_ring(nb, 1)), pp(kv_p[h:], "blk", y_ring(nb, -1))]

    q1, kv1, give1 = project_stage(where, w, scale, [a_m, a_p], [], (), done, None, False)
    q1x, kv1 = swap(kv1, give1)
    part, kv1 = hold((part, kv1))
    part = project_part(where, w, [b_m, b_p], (1, 2), part)
    kv1_near = near_y(kv1)
    q2, kv2, give2 = project_stage(where, w, scale, [a0, a1], [b0, b1], (3, 3), None, part, True)
    give2, kv1_near = hold((give2, kv1_near))
    q2x, kv2 = swap(kv2, give2)
    kv2_near = near_y(kv2)
    q = jnp.concatenate([q1, q2, q1x, q2x], axis=0)
    kv2_far = far_y(*kv2_near)

    big = (512, 512, 256)
    state = attention(q, bias, [kv1] + kv1_near + [kv2], ((768,),) * 3 + (big,), 0, None, False)
    state, kv1_near = hold((state, kv1_near))
    kv1_far = far_y(*kv1_near)
    state = attention(q, bias, kv2_near + kv1_far, (big, big, (384,), (384,)), 28, state, False)
    out = attention(q, bias, kv2_far, ((384, 256),) * 2, 54, state, True)

    out = out.reshape(2, 2, nu, half, HD)
    other = pp(out[1], "blk", core_swap(nb))
    mine = out[0]
    first = jnp.where(core == 0, mine, other)
    second = jnp.where(core == 0, other, mine)
    heads = jnp.concatenate([first, second], axis=-1)
    heads = [heads[:, g].reshape(2 * half, 2 * HD) for g in range(nu)]
    arrived = [heads[0]] + [
        pp(heads[i], "ulysses", ring(nu, OFFSETS[i])) for i in range(1, nu)
    ]
    w_o = load_columns(where, w_out, heads[0])
    bf = jnp.bfloat16
    far_0, far_1 = out_project(where, arrived, w_o, (3,), bf, 2)
    rows = 2 * half
    hr = rows // 2
    far_m = pp(far_0, "tensor", ring(nt, 1))
    far_p = pp(far_1, "tensor", ring(nt, -1))
    (to_m,) = out_project(where, arrived, w_o, (1,), jnp.float32, 1)
    (to_p,) = out_project(where, arrived, w_o, (2,), jnp.float32, 1)
    to_p = jnp.concatenate([to_p[:hr] + far_m.astype(jnp.float32), to_p[hr:]], axis=0).astype(bf)
    to_m = jnp.concatenate([to_m[:hr], to_m[hr:] + far_p.astype(jnp.float32)], axis=0).astype(bf)
    from_m = pp(to_p, "tensor", ring(nt, 1))
    from_p = pp(to_m, "tensor", ring(nt, -1))
    (own,) = out_project(where, arrived, w_o, (0,), jnp.float32, 1)
    return (own + from_m.astype(jnp.float32) + from_p.astype(jnp.float32)).astype(bf)


def solution(mesh):
    return jax.shard_map(
        local,
        mesh=mesh,
        in_specs=(
            P(("ulysses", "blk"), "tensor"),
            P(None, None, ("ulysses", "tensor")),
            P(None, ("ulysses", "tensor")),
            P(("ulysses", "tensor"), None, None),
            P(None, "tensor", None),
        ),
        out_specs=P(("ulysses", "blk"), "tensor"),
        check_vma=False,
    )
```
